32 devices in a mesh: group: 4 (over y, core), ingroup: 4 (over z), dp: 2 (over x).
Axes of the slice: x: 2, y: 2, z: 4, core: 2. Of those that a mesh axis runs over, the one named last changes fastest.
Arguments:
- tokens: bfloat16 [256, 3584], P(('group', 'ingroup'), 'dp'), may hold values from -6 to 6
- cotangent: bfloat16 [256, 3584], P(('group', 'ingroup'), 'dp'), may hold values from -6 to 6
- expert_ids: int32 [256, 8], P(('group', 'ingroup')), may hold values from 0 to 15, as said below
- gate_fixed: int32 [256, 8], P(('group', 'ingroup')), may hold values from 6554 to 65535
- w_gate: bfloat16 [16, 3584, 1024], P(('group', 'ingroup'), 'dp'), may hold values from -0.09375 to 0.09375
- w_up: bfloat16 [16, 3584, 1024], P(('group', 'ingroup'), 'dp'), may hold values from -0.09375 to 0.09375
- w_down: bfloat16 [16, 1024, 3584], P(('group', 'ingroup'), None, 'dp'), may hold values from -0.1875 to 0.1875
Outputs:
- mixed: bfloat16 [256, 3584], P(('group', 'ingroup'), 'dp')
- token_grad: bfloat16 [256, 3584], P(('group', 'ingroup'), 'dp')
The draws below stay inside these ranges and needn't reach their ends.
Inputs may be any that keep to these rules, and one draw needn't show every extreme that they name: `expert_ids`: expert e belongs to group e // 4. Each token chooses 4 different groups and names two experts in each, 8 different experts in all. One group, drawn from the seed, is chosen by every token. In each aligned block of 16 tokens at most 8 tokens name one expert, and the experts of one group are named by counts that differ by at most one.
All inputs are finite; a program needn't handle non-finite values.
Results may differ from the reference program's by a relative error of at most 0.0064.
Values may be sent and summed in bfloat16 or wider, within the bound.
No kernel may reach another device: no remote copies, remote signals or barrier semaphores. Data moves between devices by JAX's collectives and lax.ppermute only.
A program may use at most 64 MiB of HBM per device.

```python
import jax
import jax.numpy as jnp
from jax import lax

D = 3584
FFW = 1024
TOK_DEV = 16
TOPK = 8
TOPG = 4
EXPERTS = 16
ROWS = 128
TOKENS = 256
N_GROUP = 4
N_INGROUP = 4


def draw_expert_ids(key, part):
    block_count = N_GROUP * N_INGROUP
    hot_key = jax.random.fold_in(key, 11)
    score_key = jax.random.fold_in(key, 12)
    order_key = jax.random.fold_in(key, 13)
    hot_group = jax.random.randint(hot_key, (), 0, N_GROUP)
    group_ids = jnp.arange(N_GROUP, dtype=jnp.int32)
    scores = jax.random.randint(score_key, (block_count, TOK_DEV, N_GROUP), 0, 1 << 20) * N_GROUP + group_ids
    scores = jnp.where(group_ids == hot_group, -1, scores)
    chosen = jnp.argsort(scores, axis=-1)[..., :TOPG].astype(jnp.int32)
    picked = jnp.sum((chosen[..., None] == group_ids).astype(jnp.int32), axis=2)
    before = jnp.cumsum(picked, axis=1) - picked
    turn_index = jnp.take_along_axis(before, chosen, axis=2)
    inner_ids = jnp.arange(N_INGROUP, dtype=jnp.int32)
    order_scores = jax.random.randint(order_key, (block_count, N_GROUP, N_INGROUP), 0, 1 << 20) * N_INGROUP + inner_ids
    orders = jnp.argsort(order_scores, axis=-1).astype(jnp.int32)
    spread = jnp.broadcast_to(orders[:, None], (block_count, TOK_DEV, N_GROUP, N_INGROUP))
    own_order = jnp.take_along_axis(spread, jnp.broadcast_to(chosen[..., None], (block_count, TOK_DEV, TOPG, N_INGROUP)), axis=2)
    first_pick = jnp.take_along_axis(own_order, (2 * turn_index % N_INGROUP)[..., None], axis=3)
    second = jnp.take_along_axis(own_order, ((2 * turn_index + 1) % N_INGROUP)[..., None], axis=3)
    members = jnp.concatenate([first_pick, second], axis=3)
    named = chosen[..., None] * N_INGROUP + members
    return named.reshape(block_count * TOK_DEV, TOPK).astype(jnp.int32)


def with_ends(result, key, least, high):
    shape = result.shape
    place = [jax.random.randint(jax.random.fold_in(key, axis), (), 0, shape[axis]) for axis in range(len(shape))]
    result = result.at[tuple(place)].set(least)
    longest = shape.index(max(shape))
    place[longest] = (place[longest] + 1) % shape[longest]
    return result.at[tuple(place)].set(high)


def steps_of(key, extent, pieces, least, top_value):
    level, own = 1.0, jax.random.fold_in(key, 6)
    for axis_at, parts in pieces:
        steps = jnp.exp(jax.random.uniform(jax.random.fold_in(own, axis_at), (parts,), jnp.float32, least / len(pieces), top_value / len(pieces)))
        level = level * jnp.repeat(steps, extent[axis_at] // parts).reshape([-1 if axis == axis_at else 1 for axis in range(len(extent))])
    return level


def normal_values(key, dims, scale, limit, shards=(), held_as=jnp.bfloat16):
    values = jax.random.normal(key, dims, jnp.float32) * scale
    if len(shards) > 0:
        values = steps_of(key, dims, shards, -0.22, 0.18) * values
    return jnp.clip(values, min=-limit, max=limit).astype(held_as)


def setup_inputs(seed: int = 0) -> dict:
    keys = jax.random.split(jax.random.key(seed), 8)
    return {
        "tokens": normal_values(keys[0], (TOKENS, D), 1.0, 6.0, ((0, 16), (1, 2))),
        "cotangent": normal_values(keys[1], (TOKENS, D), 1.0, 6.0, ((0, 16), (1, 2))),
        "expert_ids": draw_expert_ids(jax.random.fold_in(keys[7], 71), 0),
        "gate_fixed": with_ends(jax.random.randint(keys[3], (TOKENS, TOPK), 6554, 65536), jax.random.fold_in(keys[3], 1), 6554, 65535).astype(jnp.int32),
        "w_gate": normal_values(keys[4], (EXPERTS, D, FFW), D ** -0.5, 0.09375, ((0, 16), (1, 2))),
        "w_up": normal_values(keys[5], (EXPERTS, D, FFW), D ** -0.5, 0.09375, ((0, 16), (1, 2))),
        "w_down": normal_values(keys[6], (EXPERTS, FFW, D), FFW ** -0.5, 0.1875, ((0, 16), (2, 2))),
    }


def reference(tokens, cotangent, expert_ids, gate_fixed, w_gate, w_up, w_down):
    flat_ids = expert_ids.reshape(-1)
    gate_scale = gate_fixed.reshape(-1).astype(jnp.float32) / 65536.0

    def per_expert(totals, expert):
        mixed_sum, grad_sum = totals
        matches = flat_ids == expert
        positions = jnp.nonzero(matches, size=ROWS, fill_value=0)[0].astype(jnp.int32)
        is_valid = matches[positions]
        owner_row = positions // TOPK
        row_scale = jnp.where(is_valid, gate_scale[positions], jnp.float32(0.0))
        row_data = jnp.where(is_valid[:, None], tokens[owner_row], jnp.zeros((), tokens.dtype))
        scaled_cot = (row_scale[:, None] * cotangent[owner_row].astype(jnp.float32)).astype(jnp.bfloat16)
        gate_weight = w_gate[expert]
        up_weight = w_up[expert]
        down_weight = w_down[expert]
        gate_pre = jnp.dot(row_data, gate_weight, preferred_element_type=jnp.float32)
        up_pre = jnp.dot(row_data, up_weight, preferred_element_type=jnp.float32)
        hidden = (jax.nn.silu(gate_pre) * up_pre).astype(jnp.bfloat16)
        expert_out = jnp.dot(hidden, down_weight, preferred_element_type=jnp.float32).astype(jnp.bfloat16)
        d_hidden = jnp.dot(scaled_cot, down_weight.T, preferred_element_type=jnp.float32)
        sigmoid_gate = jax.nn.sigmoid(gate_pre)
        d_gate = (d_hidden * up_pre * sigmoid_gate * (1.0 + gate_pre * (1.0 - sigmoid_gate))).astype(jnp.bfloat16)
        d_up = (d_hidden * jax.nn.silu(gate_pre)).astype(jnp.bfloat16)
        expert_grad = (jnp.dot(d_gate, gate_weight.T, preferred_element_type=jnp.float32)
                       + jnp.dot(d_up, up_weight.T, preferred_element_type=jnp.float32)).astype(jnp.bfloat16)
        mixed_sum = mixed_sum.at[owner_row].add(row_scale[:, None] * expert_out.astype(jnp.float32))
        grad_sum = grad_sum.at[owner_row].add(jnp.where(is_valid[:, None], expert_grad.astype(jnp.float32), jnp.float32(0.0)))
        return (mixed_sum, grad_sum), None

    zero_sums = jnp.zeros(tokens.shape, jnp.float32)
    (mixed_sum, grad_sum), unused = lax.scan(per_expert, (zero_sums, zero_sums), jnp.arange(EXPERTS, dtype=jnp.int32))
    return mixed_sum.astype(jnp.bfloat16), grad_sum.astype(jnp.bfloat16)
```

```python
import jax
import jax.numpy as jnp
from jax import lax
from jax.sharding import PartitionSpec as P

PLANE = ("group", "ingroup")


def dot(left, right, left_dim=1, right_dim=0):
    return lax.dot_general(
        left,
        right,
        (((left_dim,), (right_dim,)), ((), ())),
        preferred_element_type=jnp.float32,
    )


def dp_total(part):
    count = lax.axis_size("dp")
    sent = part.astype(jnp.bfloat16)
    total = part
    for step in range(1, count):
        pairs = [(i, (i + step) % count) for i in range(count)]
        total = total + lax.ppermute(sent, "dp", pairs).astype(jnp.float32)
    return total


def on_device(tokens, cotangent, expert_ids, gate_fixed, w_gate, w_up, w_down):
    group_count = lax.axis_size("group")
    inner_count = lax.axis_size("ingroup")
    block, features = tokens.shape
    expert_count = group_count * inner_count
    capacity = 2 * block // inner_count
    slots = expert_count * capacity
    total = expert_count * block

    routing = gate_fixed * expert_count + expert_ids
    routing = lax.all_gather(routing, PLANE, axis=0, tiled=True)
    all_x = lax.all_gather(tokens, PLANE, axis=0, tiled=True)
    all_d = lax.all_gather(cotangent, PLANE, axis=0, tiled=True)

    me = lax.axis_index(PLANE)
    match = (routing % expert_count) == me
    named = jnp.any(match, axis=1)
    gate = jnp.sum(jnp.where(match, routing // expert_count, 0), axis=1)
    index = jnp.arange(total, dtype=jnp.int32)
    earlier = ((index[:, None] // block) == (index[None, :] // block)) & (
        index[:, None] > index[None, :]
    )
    named_cols = jnp.broadcast_to(named[:, None], (total, slots)).astype(jnp.bfloat16)
    rank = dot(earlier.astype(jnp.bfloat16), named_cols).astype(jnp.int32)
    slot = rank + (index // block * capacity)[:, None]
    place = ((slot == jnp.arange(slots, dtype=jnp.int32)) & named[:, None]).astype(jnp.bfloat16)
    halves = jnp.stack([gate // 256, gate % 256], axis=1).astype(jnp.bfloat16)
    row_halves = dot(place, halves, 0, 0)
    scale = (row_halves[:, :1] * 256.0 + row_halves[:, 1:]) / 65536.0

    rows_x = dot(place, all_x, 0, 0).astype(jnp.bfloat16)
    rows_d = dot(place, all_d, 0, 0).astype(jnp.bfloat16)
    gate_pre = dp_total(dot(rows_x, w_gate[0]))
    up_pre = dp_total(dot(rows_x, w_up[0]))
    d_hidden = dp_total(dot(rows_d, w_down[0], 1, 1)) * scale
    sigmoid = jax.nn.sigmoid(gate_pre)
    hidden = (gate_pre * sigmoid * up_pre).astype(jnp.bfloat16)
    d_gate = (d_hidden * up_pre * sigmoid * (1.0 + gate_pre * (1.0 - sigmoid))).astype(jnp.bfloat16)
    d_up = (d_hidden * gate_pre * sigmoid).astype(jnp.bfloat16)
    out_rows = (dot(hidden, w_down[0]) * scale).astype(jnp.bfloat16)
    grad_rows = (dot(d_gate, w_gate[0], 1, 1) + dot(d_up, w_up[0], 1, 1)).astype(jnp.bfloat16)
    mixed = lax.psum_scatter(
        dot(place, out_rows).astype(jnp.bfloat16), PLANE, scatter_dimension=0, tiled=True
    )
    grad = lax.psum_scatter(
        dot(place, grad_rows).astype(jnp.bfloat16), PLANE, scatter_dimension=0, tiled=True
    )
    return mixed, grad


def solution(mesh):
    rows = P(PLANE, "dp")
    placed = (
        rows,
        rows,
        P(PLANE, None),
        P(PLANE, None),
        P(PLANE, "dp", None),
        P(PLANE, "dp", None),
        P(PLANE, None, "dp"),
    )
    return jax.shard_map(
        on_device, mesh=mesh, in_specs=placed, out_specs=(rows, rows), check_vma=False
    )
```

```python
import jax
import jax.numpy as jnp
from jax import lax
from jax.sharding import PartitionSpec as P

PLANE = ("group", "ingroup")
LANES = 128


def dot(left, right, left_dim=1, right_dim=0):
    return lax.dot_general(
        left,
        right,
        (((left_dim,), (right_dim,)), ((), ())),
        preferred_element_type=jnp.float32,
    )


def swap(value, axis, offset):
    return lax.ppermute(value, axis, [(i, i ^ offset) for i in range(lax.axis_size(axis))])


def group_bits():
    bits, bit = [], lax.axis_size("group") // 2
    while bit:
        bits.append(bit)
        bit //= 2
    return bits


def spread(own):
    bits = group_bits()
    inner = [own] + [swap(own, "ingroup", j) for j in range(1, lax.axis_size("ingroup"))]
    early = swap(own, "group", bits[0])
    rest = jnp.concatenate(inner[1:], axis=0)
    late = swap(rest, "group", bits[0])
    parts = [own, rest, early, late]
    for bit in bits[1:]:
        held = parts
        near = jnp.concatenate(held[: len(held) // 2], axis=0)
        far = jnp.concatenate(held[len(held) // 2 :], axis=0)
        parts = [near, far, swap(near, "group", bit), swap(far, "group", bit)]
    return jnp.concatenate(parts, axis=0)


def gather_sum(terms, block):
    for bit in reversed(group_bits()[1:]):
        half = terms.shape[0] // 2
        received = swap(terms[half:].astype(jnp.bfloat16), "group", bit)
        terms = terms[:half] + received.astype(jnp.float32)
    half = terms.shape[0] // 2
    first_bit = group_bits()[0]
    late = swap(terms[half + block :].astype(jnp.bfloat16), "group", first_bit)
    early = swap(terms[half : half + block].astype(jnp.bfloat16), "group", first_bit)
    away = (terms[block:half] + late.astype(jnp.float32)).astype(jnp.bfloat16)
    total = terms[:block] + early.astype(jnp.float32)
    for j in range(1, lax.axis_size("ingroup")):
        total = total + swap(away[(j - 1) * block : j * block], "ingroup", j).astype(jnp.float32)
    return total.astype(jnp.bfloat16)


def dp_total(part):
    count = lax.axis_size("dp")
    sent = part.astype(jnp.bfloat16)
    total = part
    for step in range(1, count):
        pairs = [(i, (i + step) % count) for i in range(count)]
        total = total + lax.ppermute(sent, "dp", pairs).astype(jnp.float32)
    return total


def on_device(tokens, cotangent, expert_ids, gate_fixed, w_gate, w_up, w_down):
    group_count = lax.axis_size("group")
    inner_count = lax.axis_size("ingroup")
    block, features = tokens.shape
    topk = expert_ids.shape[1]
    expert_count = group_count * inner_count
    capacity = 2 * block // inner_count
    slots = expert_count * capacity
    total = expert_count * block

    routing = jnp.concatenate([expert_ids, gate_fixed // 256, gate_fixed % 256], axis=1)
    routing = jnp.pad(routing, ((0, 0), (0, LANES - 3 * topk))).astype(jnp.bfloat16)
    all_x = spread(jnp.concatenate([tokens, routing], axis=1))
    all_d = spread(cotangent)

    me = lax.axis_index(PLANE).astype(jnp.float32)
    routing = all_x[:, features:].astype(jnp.float32)
    match = routing[:, :topk] == me
    high = jnp.sum(jnp.where(match, routing[:, topk : 2 * topk], 0.0), axis=1)
    low = jnp.sum(jnp.where(match, routing[:, 2 * topk : 3 * topk], 0.0), axis=1)
    named = jnp.any(match, axis=1)
    index = jnp.arange(total, dtype=jnp.int32)
    earlier = ((index[:, None] // block) == (index[None, :] // block)) & (
        index[:, None] > index[None, :]
    )
    named_cols = jnp.broadcast_to(named[:, None], (total, slots)).astype(jnp.bfloat16)
    rank = dot(earlier.astype(jnp.bfloat16), named_cols).astype(jnp.int32)
    slot = rank + (index // block * capacity)[:, None]
    place = ((slot == jnp.arange(slots, dtype=jnp.int32)) & named[:, None]).astype(jnp.bfloat16)
    halves = jnp.stack([high, low], axis=1).astype(jnp.bfloat16)
    row_halves = dot(place, halves, 0, 0)
    scale = (row_halves[:, :1] * 256.0 + row_halves[:, 1:]) / 65536.0

    rows_x = dot(place, all_x[:, :features], 0, 0).astype(jnp.bfloat16)
    rows_d = dot(place, all_d, 0, 0).astype(jnp.bfloat16)
    gate_pre = dp_total(dot(rows_x, w_gate[0]))
    up_pre = dp_total(dot(rows_x, w_up[0]))
    d_hidden = dp_total(dot(rows_d, w_down[0], 1, 1)) * scale
    sigmoid = jax.nn.sigmoid(gate_pre)
    hidden = (gate_pre * sigmoid * up_pre).astype(jnp.bfloat16)
    d_gate = (d_hidden * up_pre * sigmoid * (1.0 + gate_pre * (1.0 - sigmoid))).astype(jnp.bfloat16)
    d_up = (d_hidden * gate_pre * sigmoid).astype(jnp.bfloat16)
    out_rows = (dot(hidden, w_down[0]) * scale).astype(jnp.bfloat16)
    grad_rows = (dot(d_gate, w_gate[0], 1, 1) + dot(d_up, w_up[0], 1, 1)).astype(jnp.bfloat16)
    return gather_sum(dot(place, out_rows), block), gather_sum(dot(place, grad_rows), block)


def solution(mesh):
    rows = P(PLANE, "dp")
    placed = (
        rows,
        rows,
        P(PLANE, None),
        P(PLANE, None),
        P(PLANE, "dp", None),
        P(PLANE, "dp", None),
        P(PLANE, None, "dp"),
    )
    return jax.shard_map(
        on_device, mesh=mesh, in_specs=placed, out_specs=(rows, rows), check_vma=False
    )
```

```python
import functools

import jax
import jax.numpy as jnp
from jax import lax
from jax.experimental import pallas as pl
from jax.experimental.pallas import tpu as pltpu
from jax.sharding import PartitionSpec as P

PLANE = ("group", "ingroup")
LANES = 128
CHUNK = 256
BF16 = jnp.bfloat16
F32 = jnp.float32


def dot(left, right, left_dim=1, right_dim=0):
    return lax.dot_general(
        left, right, (((left_dim,), (right_dim,)), ((), ())), preferred_element_type=F32
    )


def call(body, outs, args, flops=0, limit=16):
    shapes = [jax.ShapeDtypeStruct(shape, dtype) for shape, dtype in outs]
    moved = sum(a.size * a.dtype.itemsize for a in args)
    moved += sum(s.size * s.dtype.itemsize for s in shapes)
    specs = [
        pl.BlockSpec(memory_space=pltpu.SMEM if a.shape == (1,) else pltpu.VMEM) for a in args
    ]
    return pl.pallas_call(
        body,
        out_shape=shapes,
        in_specs=specs,
        out_specs=[pl.BlockSpec(memory_space=pltpu.VMEM)] * len(shapes),
        compiler_params=pltpu.CompilerParams(vmem_limit_bytes=limit << 20),
        cost_estimate=pl.CostEstimate(flops=flops, bytes_accessed=moved, transcendentals=0),
    )(*args)


def swap(value, axis, offset):
    return lax.ppermute(value, axis, [(i, i ^ offset) for i in range(lax.axis_size(axis))])


def bits_of(axis):
    bits, bit = [], lax.axis_size(axis) // 2
    while bit:
        bits.append(bit)
        bit //= 2
    return bits


def payload_body(wide, tokens, ids, gate, out):
    topk, block = ids.shape
    features = tokens.shape[1]
    rows = jnp.concatenate(
        [
            ids[...].astype(F32),
            (gate[...] >> 8).astype(F32),
            (gate[...] & 255).astype(F32),
            jnp.zeros((LANES - 3 * topk, block), F32),
        ],
        axis=0,
    ).astype(BF16)
    eye = lax.broadcasted_iota(jnp.int32, (block, block), 0) == lax.broadcasted_iota(
        jnp.int32, (block, block), 1
    )
    if wide != features:
        out[...] = jnp.zeros_like(out)
    out[:, :features] = tokens[...]
    out[:, wide:] = dot(jnp.where(eye, 1.0, 0.0).astype(BF16), rows, 1, 1).astype(BF16)


def pack_body(count, *refs):
    parts, out = refs[:count], refs[-1]
    at = 0
    for part in parts:
        out[at : at + part.shape[0]] = part[...]
        at += part.shape[0]


def pack_with_body(left, right, other, out, other_out):
    out[: left.shape[0]] = left[...]
    out[left.shape[0] :] = right[...]
    other_out[...] = other[...]


def pack(parts):
    rows = sum(p.shape[0] for p in parts)
    shape = (rows, parts[0].shape[1])
    return call(functools.partial(pack_body, len(parts)), [(shape, parts[0].dtype)], parts)[0]


def spread(own, follower=None):
    inner, outer = bits_of("ingroup"), bits_of("group")
    current = own
    for bit in inner[:-1]:
        received = swap(current, "ingroup", bit)
        if follower is not None and current is own:
            shape = (2 * own.shape[0], own.shape[1])
            current, follower = call(
                pack_with_body,
                [(shape, own.dtype), (follower.shape, follower.dtype)],
                [current, received, follower],
            )
        else:
            current = pack([current, received])
    beside = swap(current, "ingroup", inner[-1])
    across = swap(current, "group", outer[0])
    last = swap(beside, "group", outer[0])
    held = [current, beside, across, last]
    for bit in outer[1:]:
        held = held + [swap(pack(held[:-1]), "group", bit), swap(held[-1], "group", bit)]
    return held, follower


def route_body(wide, topk, block, capacity, count, me, *refs):
    parts, (weight, place_out, scale_out, rows_out, part_out, sent_out) = (
        refs[:count],
        refs[count:],
    )
    features = weight.shape[0]
    total, slots = place_out.shape
    routing = jnp.concatenate([p[:, wide : wide + LANES] for p in parts], axis=0)
    lane = lax.broadcasted_iota(jnp.int32, (total, LANES), 1)
    match = (routing.astype(F32) == me[0].astype(F32)) & (lane < topk)
    source = lax.broadcasted_iota(jnp.int32, (LANES, LANES), 0)
    target = lax.broadcasted_iota(jnp.int32, (LANES, LANES), 1)

    def gate_half(offset):
        moved = dot(routing, jnp.where(source == target + offset, 1.0, 0.0).astype(BF16))
        own = jnp.where(match, moved, 0.0).astype(BF16)
        return dot(own, jnp.ones((LANES, LANES), BF16)).astype(BF16)

    named = dot(jnp.where(match, 1.0, 0.0).astype(BF16), jnp.ones((LANES, slots), BF16))
    chunk = min(total, CHUNK)
    row = lax.broadcasted_iota(jnp.int32, (chunk, chunk), 0)
    col = lax.broadcasted_iota(jnp.int32, (chunk, chunk), 1)
    earlier = jnp.where((row // block == col // block) & (row > col), 1.0, 0.0).astype(BF16)
    named_half = named.astype(BF16)
    rank = jnp.concatenate(
        [dot(earlier, named_half[i : i + chunk]) for i in range(0, total, chunk)], axis=0
    )
    start = lax.broadcasted_iota(jnp.int32, (total, slots), 0) // block * capacity
    slot = lax.broadcasted_iota(jnp.int32, (total, slots), 1) - start
    place = jnp.where((named > 0.5) & (rank == slot.astype(F32)), 1.0, 0.0).astype(BF16)
    place_out[...] = place
    high = dot(place, gate_half(topk), 0, 0)
    low = dot(place, gate_half(2 * topk), 0, 0)
    scale_out[...] = (high * 256.0 + low) / 65536.0
    values = jnp.concatenate([p[:, :features] for p in parts], axis=0)
    rows = dot(place, values, 0, 0).astype(BF16)
    rows_out[...] = rows
    part = dot(rows, weight[...])
    part_out[...] = part
    sent_out[...] = part.astype(BF16)


def up_body(rows, weight, part_out, sent_out):
    part = dot(rows[...], weight[...])
    part_out[...] = part
    sent_out[...] = part.astype(BF16)


def back_body(count, *refs):
    parts, (place, weight, part_out, sent_out) = refs[:count], refs[count:]
    values = jnp.concatenate([p[...] for p in parts], axis=0)
    rows = dot(place[...], values, 0, 0).astype(BF16)
    part = dot(rows, weight[...], 1, 1)
    part_out[...] = part
    sent_out[...] = part.astype(BF16)


def summed(own, received):
    total = own[...]
    for r in received:
        total = total + r[...].astype(F32)
    return total


def place_rows(place, rows, near_out, far_out):
    half = near_out.shape[0]
    near_out[...] = dot(place[:half], rows)
    far_out[...] = dot(place[half:], rows).astype(BF16)


def out_body(peers, *refs):
    gate, up = refs[0], refs[1]
    gate_in, up_in = refs[2 : 2 + peers], refs[2 + peers : 2 + 2 * peers]
    scale, place, weight, near_out, far_out = refs[2 + 2 * peers :]
    gate_pre, up_pre = summed(gate, gate_in), summed(up, up_in)
    hidden = (gate_pre / (1.0 + jnp.exp(-gate_pre)) * up_pre).astype(BF16)
    rows = (dot(hidden, weight[...]) * scale[:, :1]).astype(BF16)
    place_rows(place, rows, near_out, far_out)


def grad_body(peers, *refs):
    gate, up, back = refs[:3]
    gate_in, up_in, back_in = (refs[3 + i * peers : 3 + (i + 1) * peers] for i in range(3))
    scale, place, gate_weight, up_weight, near_out, far_out = refs[3 + 3 * peers :]
    gate_pre, up_pre = summed(gate, gate_in), summed(up, up_in)
    d_hidden = summed(back, back_in) * scale[:, :1]
    sigmoid = 1.0 / (1.0 + jnp.exp(-gate_pre))
    d_gate = (d_hidden * up_pre * sigmoid * (1.0 + gate_pre * (1.0 - sigmoid))).astype(BF16)
    d_up = (d_hidden * gate_pre * sigmoid).astype(BF16)
    rows = (dot(d_gate, gate_weight[...], 1, 1) + dot(d_up, up_weight[...], 1, 1)).astype(BF16)
    place_rows(place, rows, near_out, far_out)


def fold_body(count, cuts, keep, *refs):
    total = keep[...]
    for received in refs[:count]:
        total = total + received[...].astype(F32)
    for (start, stop, dtype), out in zip(cuts, refs[count:]):
        out[...] = total[start:stop].astype(dtype)


def fold(keep, received, cuts):
    outs = [((stop - start, keep.shape[1]), dtype) for start, stop, dtype in cuts]
    return call(
        functools.partial(fold_body, len(received), cuts), outs, [keep] + list(received)
    )


def collect(near, far):
    inner, outer = bits_of("ingroup"), bits_of("group")
    for bit in reversed(outer[2:]):
        half = near.shape[0] // 2
        near, far = fold(
            near, [swap(far, "group", bit)], [(0, half, F32), (half, 2 * half, BF16)]
        )
    half = near.shape[0] // 2
    quarter = half // 2
    received = swap(far, "group", outer[1])
    first, second, keep_far, keep_near = fold(
        near,
        [received],
        [
            (half + quarter, 2 * half, BF16),
            (half, half + quarter, BF16),
            (quarter, half, F32),
            (0, quarter, F32),
        ],
    )
    across = swap(first, "group", outer[0])
    last = swap(second, "group", outer[0])
    (far,) = fold(keep_far, [across], [(0, quarter, BF16)])
    near, received = keep_near, [last, swap(far, "ingroup", inner[-1])]
    for bit in reversed(inner[:-1]):
        half = near.shape[0] // 2
        near, far = fold(near, received, [(0, half, F32), (half, 2 * half, BF16)])
        received = [swap(far, "ingroup", bit)]
    return fold(near, received, [(0, near.shape[0], BF16)])[0]


def from_peers(sent):
    count = lax.axis_size("dp")
    return [
        lax.ppermute(sent, "dp", [(i, (i + step) % count) for i in range(count)])
        for step in range(1, count)
    ]


def on_device(tokens, cotangent, expert_ids, gate_fixed, w_gate, w_up, w_down):
    experts = lax.axis_size("group") * lax.axis_size("ingroup")
    block, features = tokens.shape
    topk = expert_ids.shape[1]
    hidden = w_gate.shape[2]
    capacity = 2 * block // lax.axis_size("ingroup")
    slots, total = experts * capacity, experts * block
    wide = -(-features // LANES) * LANES
    peers = lax.axis_size("dp") - 1
    w_gate, w_up, w_down = w_gate[0], w_up[0], w_down[0]
    product = 2 * slots * features * hidden

    (own,) = call(
        functools.partial(payload_body, wide),
        [((block, wide + LANES), BF16)],
        [tokens, expert_ids.T, gate_fixed.T],
    )
    x_parts, cotangent = spread(own, cotangent)
    d_parts, _ = spread(cotangent)
    me = lax.axis_index(PLANE).astype(jnp.int32).reshape(1)
    sums = [((slots, hidden), F32), ((slots, hidden), BF16)]
    place, scale, rows, gate, gate_sent = call(
        functools.partial(route_body, wide, topk, block, capacity, len(x_parts)),
        [((total, slots), BF16), ((slots, LANES), F32), ((slots, features), BF16)] + sums,
        [me] + x_parts + [w_gate],
        product,
    )
    gate_in = from_peers(gate_sent)
    up, up_sent = call(up_body, sums, [rows, w_up], product)
    up_in = from_peers(up_sent)
    back, back_sent = call(
        functools.partial(back_body, len(d_parts)), sums, d_parts + [place, w_down], product
    )
    back_in = from_peers(back_sent)
    halves = [((total // 2, features), F32), ((total // 2, features), BF16)]
    mixed = collect(
        *call(
            functools.partial(out_body, peers),
            halves,
            [gate, up] + gate_in + up_in + [scale, place, w_down],
            product,
        )
    )
    grad = collect(
        *call(
            functools.partial(grad_body, peers),
            halves,
            [gate, up, back] + gate_in + up_in + back_in + [scale, place, w_gate, w_up],
            2 * product,
            24,
        )
    )
    return mixed, grad


def solution(mesh):
    rows = P(PLANE, "dp")
    placed = (
        rows,
        rows,
        P(PLANE, None),
        P(PLANE, None),
        P(PLANE, "dp", None),
        P(PLANE, "dp", None),
        P(PLANE, None, "dp"),
    )
    return jax.shard_map(
        on_device, mesh=mesh, in_specs=placed, out_specs=(rows, rows), check_vma=False
    )
```

```python
import functools

import jax
import jax.numpy as jnp
from jax import lax
from jax.experimental import pallas as pl
from jax.experimental.pallas import tpu as pltpu
from jax.sharding import PartitionSpec as P

PLANE = ("group", "ingroup")
LANES = 128
CHUNK = 256
BF16 = jnp.bfloat16
F32 = jnp.float32


def dot(left, right, left_dim=1, right_dim=0):
    return lax.dot_general(
        left, right, (((left_dim,), (right_dim,)), ((), ())), preferred_element_type=F32
    )


def call(name, body, outs, args, flops=0, limit=16, hbm=(), passed=(), scratch=(), weight=1):
    shapes = [jax.ShapeDtypeStruct(shape, dtype) for shape, dtype in outs]
    moved = sum(a.size * a.dtype.itemsize for a in args)
    moved += sum(s.size * s.dtype.itemsize for s in shapes)
    specs = [
        pl.BlockSpec(
            memory_space=pltpu.HBM if i in hbm else pltpu.SMEM if a.shape == (1,) else pltpu.VMEM
        )
        for i, a in enumerate(args)
    ]
    inputs, results = len(args), len(shapes)

    def run(*refs):
        ins, rest = refs[:inputs], refs[inputs + len(passed) :]
        body(*ins, *rest[:results], *rest[results + len(passed) :])

    free = pl.BlockSpec(memory_space=pl.ANY)
    kernel = pl.pallas_call(
        run,
        out_shape=shapes + [jax.ShapeDtypeStruct(p.shape, p.dtype) for p in passed],
        in_specs=specs + [free] * len(passed),
        out_specs=[pl.BlockSpec(memory_space=pltpu.VMEM)] * results + [free] * len(passed),
        input_output_aliases={inputs + i: results + i for i in range(len(passed))},
        scratch_shapes=list(scratch),
        compiler_params=pltpu.CompilerParams(vmem_limit_bytes=limit << 20),
        name=name,
        cost_estimate=pl.CostEstimate(flops=flops, bytes_accessed=moved * weight, transcendentals=0),
    )
    with jax.named_scope(name):
        return kernel(*args, *passed)


def swap(value, axis, offset):
    return lax.ppermute(value, axis, [(i, i ^ offset) for i in range(lax.axis_size(axis))])


def bits_of(axis):
    bits, bit = [], lax.axis_size(axis) // 2
    while bit:
        bits.append(bit)
        bit //= 2
    return bits


def routing_body(ids, gate, out):
    topk, block = ids.shape
    rows = jnp.concatenate(
        [
            ids[...].astype(F32),
            (gate[...] >> 8).astype(F32),
            (gate[...] & 255).astype(F32),
            jnp.zeros((LANES - 3 * topk, block), F32),
        ],
        axis=0,
    ).astype(BF16)
    eye = lax.broadcasted_iota(jnp.int32, (block, block), 0) == lax.broadcasted_iota(
        jnp.int32, (block, block), 1
    )
    out[...] = dot(jnp.where(eye, 1.0, 0.0).astype(BF16), rows, 1, 1).astype(BF16)


def merge_body(near_x, far_x, near_route, far_route, out):
    block, features = near_x.shape
    wide = out.shape[1] - LANES
    if wide != features:
        out[...] = jnp.zeros_like(out)
    out[:block, :features] = near_x[...]
    out[block:, :features] = far_x[...]
    out[:block, wide:] = near_route[...]
    out[block:, wide:] = far_route[...]


def pack_body(count, *refs):
    parts, out = refs[:count], refs[-1]
    at = 0
    for part in parts:
        out[at : at + part.shape[0]] = part[...]
        at += part.shape[0]


def pack(parts, after=()):
    shape = (sum(p.shape[0] for p in parts), parts[0].shape[1])
    return call(
        "pack",
        functools.partial(pack_body, len(parts)),
        [(shape, parts[0].dtype)],
        list(parts) + list(after),
        weight=1,
    )[0]


def copy_body(source, after, out):
    out[...] = source[...]


def copied(source, after):
    return call("copied", copy_body, [(source.shape, source.dtype)], [source, after], weight=40)[0]


def spread(tokens, route, cotangent):
    inner, outer = bits_of("ingroup"), bits_of("group")
    block, features = tokens.shape
    wide = -(-features // LANES) * LANES
    first, second = None, copied(cotangent, route)
    first, second = call(
        "merge",
        merge_body,
        [((2 * block, wide + LANES), BF16)],
        [tokens, swap(tokens, "ingroup", inner[0]), route, swap(route, "ingroup", inner[0])],
        passed=[second],
    )
    for bit in inner[1:-1]:
        first = pack([first, swap(first, "ingroup", bit)])
    beside = swap(first, "ingroup", inner[-1])
    across = swap(first, "group", outer[0])
    last = swap(beside, "group", outer[0])
    for bit in inner[:-1]:
        second = pack([second, swap(second, "ingroup", bit)])
    first = pack([first, beside, across, last], after=[second])
    beside = swap(second, "ingroup", inner[-1])
    across = swap(second, "group", outer[0])
    last = swap(beside, "group", outer[0])
    for bit in outer[1:-1]:
        first = pack([first, swap(first, "group", bit)])
    second = pack([second, beside, across, last])
    for bit in outer[1:-1]:
        second = pack([second, swap(second, "group", bit)])
    first = [first, swap(first, "group", outer[-1])]
    return first, [second, swap(second, "group", outer[-1])]


def route_body(wide, topk, block, capacity, count, me, *refs):
    parts, (weight, place_out, scale_out, rows_out, part_out, sent_out) = (
        refs[:count],
        refs[count:],
    )
    features = weight.shape[0]
    total, slots = place_out.shape
    routing = jnp.concatenate([p[:, wide : wide + LANES] for p in parts], axis=0)
    lane = lax.broadcasted_iota(jnp.int32, (total, LANES), 1)
    match = (routing.astype(F32) == me[0].astype(F32)) & (lane < topk)
    source = lax.broadcasted_iota(jnp.int32, (LANES, LANES), 0)
    target = lax.broadcasted_iota(jnp.int32, (LANES, LANES), 1)

    def gate_half(offset):
        moved = dot(routing, jnp.where(source == target + offset, 1.0, 0.0).astype(BF16))
        own = jnp.where(match, moved, 0.0).astype(BF16)
        return dot(own, jnp.ones((LANES, LANES), BF16)).astype(BF16)

    named = dot(jnp.where(match, 1.0, 0.0).astype(BF16), jnp.ones((LANES, slots), BF16))
    chunk = min(total, CHUNK)
    row = lax.broadcasted_iota(jnp.int32, (chunk, chunk), 0)
    col = lax.broadcasted_iota(jnp.int32, (chunk, chunk), 1)
    earlier = jnp.where((row // block == col // block) & (row > col), 1.0, 0.0).astype(BF16)
    named_half = named.astype(BF16)
    rank = jnp.concatenate(
        [dot(earlier, named_half[i : i + chunk]) for i in range(0, total, chunk)], axis=0
    )
    start = lax.broadcasted_iota(jnp.int32, (total, slots), 0) // block * capacity
    slot = lax.broadcasted_iota(jnp.int32, (total, slots), 1) - start
    place = jnp.where((named > 0.5) & (rank == slot.astype(F32)), 1.0, 0.0).astype(BF16)
    place_out[...] = place
    high = dot(place, gate_half(topk), 0, 0)
    low = dot(place, gate_half(2 * topk), 0, 0)
    scale_out[...] = (high * 256.0 + low) / 65536.0
    values = jnp.concatenate([p[:, :features] for p in parts], axis=0)
    rows = dot(place, values, 0, 0).astype(BF16)
    rows_out[...] = rows
    part = dot(rows, weight[...])
    part_out[...] = part
    sent_out[...] = part.astype(BF16)


def up_body(rows, weight, part_out, sent_out):
    part = dot(rows[...], weight[...])
    part_out[...] = part
    sent_out[...] = part.astype(BF16)


def back_body(count, *refs):
    parts, (place, weight, part_out, sent_out) = refs[:count], refs[count:]
    values = jnp.concatenate([p[...] for p in parts], axis=0)
    rows = dot(place[...], values, 0, 0).astype(BF16)
    part = dot(rows, weight[...], 1, 1)
    part_out[...] = part
    sent_out[...] = part.astype(BF16)


def summed(own, received):
    total = own[...]
    for r in received:
        total = total + r[...].astype(F32)
    return total


def place_rows(place, rows, near_out, far_out):
    half = near_out.shape[0]
    near_out[...] = dot(place[:half], rows)
    far_out[...] = dot(place[half:], rows).astype(BF16)


def out_body(peers, *refs):
    gate, up = refs[0], refs[1]
    gate_in, up_in = refs[2 : 2 + peers], refs[2 + peers : 2 + 2 * peers]
    scale, place, weight, _, near_out, far_out = refs[2 + 2 * peers :]
    gate_pre, up_pre = summed(gate, gate_in), summed(up, up_in)
    hidden = (gate_pre / (1.0 + jnp.exp(-gate_pre)) * up_pre).astype(BF16)
    rows = (dot(hidden, weight[...]) * scale[:, :1]).astype(BF16)
    place_rows(place, rows, near_out, far_out)


def factor_body(peers, *refs):
    gate, up = refs[0], refs[1]
    gate_in, up_in = refs[2 : 2 + peers], refs[2 + peers : 2 + 2 * peers]
    scale, gate_out, up_out = refs[2 + 2 * peers :]
    gate_pre, up_pre = summed(gate, gate_in), summed(up, up_in)
    sigmoid = 1.0 / (1.0 + jnp.exp(-gate_pre))
    scaled = sigmoid * scale[:, :1]
    gate_out[...] = up_pre * scaled * (1.0 + gate_pre * (1.0 - sigmoid))
    up_out[...] = gate_pre * scaled


def grad_body(peers, *refs):
    gate_factor, up_factor, back = refs[:3]
    back_in = refs[3 : 3 + peers]
    place, gate_weight, up_weight, near_out, far_out = refs[3 + peers :]
    d_hidden = summed(back, back_in)
    d_gate = (d_hidden * gate_factor[...]).astype(BF16)
    d_up = (d_hidden * up_factor[...]).astype(BF16)
    rows = (dot(d_gate, gate_weight[...], 1, 1) + dot(d_up, up_weight[...], 1, 1)).astype(BF16)
    place_rows(place, rows, near_out, far_out)


def fold_body(count, cuts, keep, *refs):
    total = keep[...]
    for received in refs[:count]:
        total = total + received[...].astype(F32)
    for (start, stop, dtype), out in zip(cuts, refs[count:]):
        out[...] = total[start:stop].astype(dtype)


def fold(keep, received, cuts):
    outs = [((stop - start, keep.shape[1]), dtype) for start, stop, dtype in cuts]
    return call(
        "fold", functools.partial(fold_body, len(received), cuts), outs, [keep] + list(received)
    )


def collect(near, far):
    inner, outer = bits_of("ingroup"), bits_of("group")
    for bit in reversed(outer[2:]):
        half = near.shape[0] // 2
        near, far = fold(
            near, [swap(far, "group", bit)], [(0, half, F32), (half, 2 * half, BF16)]
        )
    half = near.shape[0] // 2
    quarter = half // 2
    received = swap(far, "group", outer[1])
    first, second, keep_far, keep_near = fold(
        near,
        [received],
        [
            (half + quarter, 2 * half, BF16),
            (half, half + quarter, BF16),
            (quarter, half, F32),
            (0, quarter, F32),
        ],
    )
    across = swap(first, "group", outer[0])
    last = swap(second, "group", outer[0])
    (far,) = fold(keep_far, [across], [(0, quarter, BF16)])
    near, received = keep_near, [last, swap(far, "ingroup", inner[-1])]
    for bit in reversed(inner[:-1]):
        half = near.shape[0] // 2
        near, far = fold(near, received, [(0, half, F32), (half, 2 * half, BF16)])
        received = [swap(far, "ingroup", bit)]
    return fold(near, received, [(0, near.shape[0], BF16)])[0]


def collect_start(near, far):
    half = near.shape[0] // 2
    received = swap(far, "group", bits_of("group")[-1])
    return fold(near, [received], [(0, half, F32), (half, 2 * half, BF16)])


def collect_rest(near, far):
    steps = [("ingroup", b) for b in bits_of("ingroup")]
    steps += [("group", b) for b in bits_of("group")[:-1]]
    while steps:
        received = swap(far, *steps.pop())
        half = near.shape[0] // 2
        if not steps:
            return fold(near, [received], [(0, near.shape[0], BF16)])[0]
        near, far = fold(near, [received], [(0, half, F32), (half, 2 * half, BF16)])


def from_peers(sent):
    count = lax.axis_size("dp")
    return [
        lax.ppermute(sent, "dp", [(i, (i + step) % count) for i in range(count)])
        for step in range(1, count)
    ]


def on_device(tokens, cotangent, expert_ids, gate_fixed, w_gate, w_up, w_down):
    experts = lax.axis_size("group") * lax.axis_size("ingroup")
    block, features = tokens.shape
    topk = expert_ids.shape[1]
    hidden = w_gate.shape[2]
    capacity = 2 * block // lax.axis_size("ingroup")
    slots, total = experts * capacity, experts * block
    wide = -(-features // LANES) * LANES
    peers = lax.axis_size("dp") - 1
    w_gate, w_up, w_down = w_gate[0], w_up[0], w_down[0]
    product = 2 * slots * features * hidden

    (route,) = call("routing", routing_body, [((block, LANES), BF16)], [expert_ids.T, gate_fixed.T])
    x_parts, d_parts = spread(tokens, route, cotangent)
    me = lax.axis_index(PLANE).astype(jnp.int32).reshape(1)
    sums = [((slots, hidden), F32), ((slots, hidden), BF16)]
    place, scale, rows, gate, gate_sent = call(
        "gate",
        functools.partial(route_body, wide, topk, block, capacity, len(x_parts)),
        [((total, slots), BF16), ((slots, LANES), F32), ((slots, features), BF16)] + sums,
        [me] + x_parts + [w_gate],
        product,
    )
    gate_in = from_peers(gate_sent)
    up, up_sent = call("up", up_body, sums, [rows, w_up], product)
    up_in = from_peers(up_sent)
    back, back_sent = call(
        "back", functools.partial(back_body, len(d_parts)), sums, d_parts + [place, w_down], product
    )
    back_in = from_peers(back_sent)
    halves = [((total // 2, features), F32), ((total // 2, features), BF16)]
    near, far = collect_start(
        *call(
            "out", functools.partial(out_body, peers),
            halves,
            [gate, up] + gate_in + up_in + [scale, place, w_down, back_sent],
            product,
        )
    )
    factors = call(
        "factor", functools.partial(factor_body, peers),
        [((slots, hidden), F32)] * 2,
        [gate, up] + gate_in + up_in + [scale],
    )
    grad = collect(
        *call(
            "grad", functools.partial(grad_body, peers),
            halves,
            list(factors) + [back] + back_in + [place, w_gate, w_up],
            2 * product,
            24,
        )
    )
    return collect_rest(near, far), grad


def solution(mesh):
    rows = P(PLANE, "dp")
    placed = (
        rows,
        rows,
        P(PLANE, None),
        P(PLANE, None),
        P(PLANE, "dp", None),
        P(PLANE, "dp", None),
        P(PLANE, None, "dp"),
    )
    return jax.shard_map(
        on_device, mesh=mesh, in_specs=placed, out_specs=(rows, rows), check_vma=False
    )
```

```python
import functools

import jax
import jax.numpy as jnp
from jax import lax
from jax.experimental import pallas as pl
from jax.experimental.pallas import tpu as pltpu
from jax.sharding import PartitionSpec as P

PLANE = ("group", "ingroup")
LANES = 128
CHUNK = 256
BF16 = jnp.bfloat16
F32 = jnp.float32


def dot(left, right, left_dim=1, right_dim=0):
    return lax.dot_general(
        left, right, (((left_dim,), (right_dim,)), ((), ())), preferred_element_type=F32
    )


def call(name, body, outs, args, flops=0, limit=16, hbm=(), passed=(), scratch=(), weight=1):
    shapes = [jax.ShapeDtypeStruct(shape, dtype) for shape, dtype in outs]
    moved = sum(a.size * a.dtype.itemsize for a in args)
    moved += sum(s.size * s.dtype.itemsize for s in shapes)
    specs = [
        pl.BlockSpec(
            memory_space=pltpu.HBM if i in hbm else pltpu.SMEM if a.shape == (1,) else pltpu.VMEM
        )
        for i, a in enumerate(args)
    ]
    inputs, results = len(args), len(shapes)

    def run(*refs):
        ins, rest = refs[:inputs], refs[inputs + len(passed) :]
        body(*ins, *rest[:results], *rest[results + len(passed) :])

    free = pl.BlockSpec(memory_space=pl.ANY)
    kernel = pl.pallas_call(
        run,
        out_shape=shapes + [jax.ShapeDtypeStruct(p.shape, p.dtype) for p in passed],
        in_specs=specs + [free] * len(passed),
        out_specs=[pl.BlockSpec(memory_space=pltpu.VMEM)] * results + [free] * len(passed),
        input_output_aliases={inputs + i: results + i for i in range(len(passed))},
        scratch_shapes=list(scratch),
        compiler_params=pltpu.CompilerParams(vmem_limit_bytes=limit << 20),
        name=name,
        cost_estimate=pl.CostEstimate(flops=flops, bytes_accessed=moved * weight, transcendentals=0),
    )
    with jax.named_scope(name):
        return kernel(*args, *passed)


def swap(value, axis, offset):
    return lax.ppermute(value, axis, [(i, i ^ offset) for i in range(lax.axis_size(axis))])


def bits_of(axis):
    bits, bit = [], lax.axis_size(axis) // 2
    while bit:
        bits.append(bit)
        bit //= 2
    return bits


def routing_body(ids, gate, out):
    topk, block = ids.shape
    rows = jnp.concatenate(
        [
            ids[...].astype(F32),
            (gate[...] >> 8).astype(F32),
            (gate[...] & 255).astype(F32),
            jnp.zeros((LANES - 3 * topk, block), F32),
        ],
        axis=0,
    ).astype(BF16)
    eye = lax.broadcasted_iota(jnp.int32, (block, block), 0) == lax.broadcasted_iota(
        jnp.int32, (block, block), 1
    )
    out[...] = dot(jnp.where(eye, 1.0, 0.0).astype(BF16), rows, 1, 1).astype(BF16)


def merge_body(near_x, far_x, near_route, far_route, out):
    block, features = near_x.shape
    wide = out.shape[1] - LANES
    if wide != features:
        out[...] = jnp.zeros_like(out)
    out[:block, :features] = near_x[...]
    out[block:, :features] = far_x[...]
    out[:block, wide:] = near_route[...]
    out[block:, wide:] = far_route[...]


def pack_body(count, *refs):
    parts, out = refs[:count], refs[-1]
    at = 0
    for part in parts:
        out[at : at + part.shape[0]] = part[...]
        at += part.shape[0]


def pack(parts, after=()):
    shape = (sum(p.shape[0] for p in parts), parts[0].shape[1])
    return call(
        "pack",
        functools.partial(pack_body, len(parts)),
        [(shape, parts[0].dtype)],
        list(parts) + list(after),
        flops=1 << 29,
    )[0]


def copy_body(source, after, out):
    out[...] = source[...]


def copied(source, after):
    return call("copied", copy_body, [(source.shape, source.dtype)], [source, after], 1 << 31)[0]


def spread(tokens, route, cotangent):
    inner, outer = bits_of("ingroup"), bits_of("group")
    block, features = tokens.shape
    wide = -(-features // LANES) * LANES
    first, second = None, copied(cotangent, route)
    first, second = call(
        "merge",
        merge_body,
        [((2 * block, wide + LANES), BF16)],
        [tokens, swap(tokens, "ingroup", inner[0]), route, swap(route, "ingroup", inner[0])],
        passed=[second],
    )
    for bit in inner[1:-1]:
        first = pack([first, swap(first, "ingroup", bit)])
    beside = swap(first, "ingroup", inner[-1])
    across = swap(first, "group", outer[0])
    last = swap(beside, "group", outer[0])
    for bit in inner[:-1]:
        second = pack([second, swap(second, "ingroup", bit)])
    first = pack([first, beside, across, last], after=[second])
    beside = swap(second, "ingroup", inner[-1])
    across = swap(second, "group", outer[0])
    last = swap(beside, "group", outer[0])
    for bit in outer[1:-1]:
        first = pack([first, swap(first, "group", bit)])
    first = [first, swap(first, "group", outer[-1])]
    return first, [second, beside, across, last]


def spread_end(parts, after):
    bits = bits_of("group")[1:]
    current = pack(parts, after)
    for bit in bits[:-1]:
        current = pack([current, swap(current, "group", bit)])
    return [current, swap(current, "group", bits[-1])]


def route_body(wide, topk, block, capacity, count, me, *refs):
    parts, (gate_weight, up_weight, place_out, scale_out, part_out, sent_out) = (
        refs[:count],
        refs[count:],
    )
    features = gate_weight.shape[0]
    total, slots = place_out.shape
    routing = jnp.concatenate([p[:, wide : wide + LANES] for p in parts], axis=0)
    lane = lax.broadcasted_iota(jnp.int32, (total, LANES), 1)
    match = (routing.astype(F32) == me[0].astype(F32)) & (lane < topk)
    source = lax.broadcasted_iota(jnp.int32, (LANES, LANES), 0)
    target = lax.broadcasted_iota(jnp.int32, (LANES, LANES), 1)

    def gate_half(offset):
        moved = dot(routing, jnp.where(source == target + offset, 1.0, 0.0).astype(BF16))
        own = jnp.where(match, moved, 0.0).astype(BF16)
        return dot(own, jnp.ones((LANES, LANES), BF16)).astype(BF16)

    named = dot(jnp.where(match, 1.0, 0.0).astype(BF16), jnp.ones((LANES, slots), BF16))
    chunk = min(total, CHUNK)
    row = lax.broadcasted_iota(jnp.int32, (chunk, chunk), 0)
    col = lax.broadcasted_iota(jnp.int32, (chunk, chunk), 1)
    earlier = jnp.where((row // block == col // block) & (row > col), 1.0, 0.0).astype(BF16)
    named_half = named.astype(BF16)
    rank = jnp.concatenate(
        [dot(earlier, named_half[i : i + chunk]) for i in range(0, total, chunk)], axis=0
    )
    start = lax.broadcasted_iota(jnp.int32, (total, slots), 0) // block * capacity
    slot = lax.broadcasted_iota(jnp.int32, (total, slots), 1) - start
    place = jnp.where((named > 0.5) & (rank == slot.astype(F32)), 1.0, 0.0).astype(BF16)
    place_out[...] = place
    high = dot(place, gate_half(topk), 0, 0)
    low = dot(place, gate_half(2 * topk), 0, 0)
    scale_out[...] = (high * 256.0 + low) / 65536.0
    values = jnp.concatenate([p[:, :features] for p in parts], axis=0)
    rows = dot(place, values, 0, 0).astype(BF16)
    for i, weight in enumerate((gate_weight, up_weight)):
        part = dot(rows, weight[...])
        part_out[i * slots : (i + 1) * slots] = part
        sent_out[i * slots : (i + 1) * slots] = part.astype(BF16)


def back_body(count, *refs):
    parts, (place, weight, part_out, sent_out) = refs[:count], refs[count:]
    values = jnp.concatenate([p[...] for p in parts], axis=0)
    rows = dot(place[...], values, 0, 0).astype(BF16)
    part = dot(rows, weight[...], 1, 1)
    part_out[...] = part
    sent_out[...] = part.astype(BF16)


def summed(own, received):
    total = own[...]
    for r in received:
        total = total + r[...].astype(F32)
    return total


def place_rows(place, rows, near_out, first_out, second_out):
    half = near_out.shape[0]
    middle = half + second_out.shape[0]
    first_out[...] = dot(place[middle:], rows).astype(BF16)
    second_out[...] = dot(place[half:middle], rows).astype(BF16)
    near_out[...] = dot(place[:half], rows)


def forward_sums(both, received):
    total = summed(both, received)
    half = total.shape[0] // 2
    return total[:half], total[half:]


def out_body(peers, *refs):
    scale, place, weight, _, near_out, first_out, second_out = refs[1 + peers :]
    gate_pre, up_pre = forward_sums(refs[0], refs[1 : 1 + peers])
    hidden = (gate_pre / (1.0 + jnp.exp(-gate_pre)) * up_pre).astype(BF16)
    rows = (dot(hidden, weight[...]) * scale[:, :1]).astype(BF16)
    place_rows(place, rows, near_out, first_out, second_out)


def factor_body(peers, *refs):
    scale, gate_out, up_out = refs[1 + peers :]
    gate_pre, up_pre = forward_sums(refs[0], refs[1 : 1 + peers])
    sigmoid = 1.0 / (1.0 + jnp.exp(-gate_pre))
    scaled = sigmoid * scale[:, :1]
    gate_out[...] = up_pre * scaled * (1.0 + gate_pre * (1.0 - sigmoid))
    up_out[...] = gate_pre * scaled


def grad_body(peers, *refs):
    gate_factor, up_factor, back = refs[:3]
    back_in = refs[3 : 3 + peers]
    place, gate_weight, up_weight, _, near_out, first_out, second_out = refs[3 + peers :]
    d_hidden = summed(back, back_in)
    d_gate = (d_hidden * gate_factor[...]).astype(BF16)
    d_up = (d_hidden * up_factor[...]).astype(BF16)
    rows = (dot(d_gate, gate_weight[...], 1, 1) + dot(d_up, up_weight[...], 1, 1)).astype(BF16)
    place_rows(place, rows, near_out, first_out, second_out)


def add_body(count, at, parts, keep, *refs):
    rows = sum(out.shape[0] for out in refs[count:])
    total = keep[at : at + rows].astype(F32)
    for received, start in zip(refs[:count], parts):
        total = total + received[start : start + rows].astype(F32)
    start = 0
    for out in refs[count:]:
        out[...] = total[start : start + out.shape[0]].astype(out.dtype)
        start += out.shape[0]


def add(keep, at, received, outs):
    return call(
        "add",
        functools.partial(add_body, len(received), at, [start for _, start in received]),
        [((rows, keep.shape[1]), dtype) for rows, dtype in outs],
        [keep] + [r for r, _ in received],
    )


def collect_start(near, first, second):
    for bit in reversed(bits_of("group")[2:]):
        half, quarter = near.shape[0] // 2, near.shape[0] // 4
        got_first, got_second = swap(first, "group", bit), swap(second, "group", bit)
        (first,) = add(near, half + quarter, [(got_first, quarter)], [(quarter, BF16)])
        (second,) = add(near, half, [(got_first, 0)], [(quarter, BF16)])
        (near,) = add(near, 0, [(got_second, 0)], [(half, F32)])
    bit = bits_of("group")[1]
    return near, swap(first, "group", bit), swap(second, "group", bit)


def collect_end(near, far, bits):
    for bit in bits:
        received = swap(far, "ingroup", bit)
        half = near.shape[0] // 2
        if bit == bits[-1]:
            return add(near, 0, [(received, 0)], [(2 * half, BF16)])[0]
        near, far = add(near, 0, [(received, 0)], [(half, F32), (half, BF16)])


def collect_few(near, far, got_second):
    inner, outer = bits_of("ingroup"), bits_of("group")
    half = near.shape[0] // 2
    quarter = half // 2
    received = swap(far, "group", outer[0])
    near, far = add(near, 0, [(got_second, 0), (received, 0)], [(quarter, F32), (quarter, BF16)])
    return collect_end(near, far, inner[::-1])


def collect_early(near, got_first, got_second):
    inner, outer = bits_of("ingroup"), bits_of("group")
    half = near.shape[0] // 2
    quarter, eighth = half // 2, half // 4
    low, high = add(near, half, [(got_first, 0)], [(quarter, BF16), (quarter, BF16)])
    across, last = swap(high, "group", outer[0]), swap(low, "group", outer[0])
    (far,) = add(near, quarter, [(got_second, quarter), (across, 0)], [(quarter, BF16)])
    beside = swap(far, "ingroup", inner[-1])
    near, far = add(
        near, 0, [(got_second, 0), (last, 0), (beside, 0)], [(eighth, F32), (eighth, BF16)]
    )
    return collect_end(near, far, inner[-2::-1])


def from_peers(sent):
    count = lax.axis_size("dp")
    return [
        lax.ppermute(sent, "dp", [(i, (i + step) % count) for i in range(count)])
        for step in range(1, count)
    ]


def on_device(tokens, cotangent, expert_ids, gate_fixed, w_gate, w_up, w_down):
    experts = lax.axis_size("group") * lax.axis_size("ingroup")
    block, features = tokens.shape
    topk = expert_ids.shape[1]
    hidden = w_gate.shape[2]
    capacity = 2 * block // lax.axis_size("ingroup")
    slots, total = experts * capacity, experts * block
    wide = -(-features // LANES) * LANES
    peers = lax.axis_size("dp") - 1
    w_gate, w_up, w_down = w_gate[0], w_up[0], w_down[0]
    product = 2 * slots * features * hidden

    (route,) = call("routing", routing_body, [((block, LANES), BF16)], [expert_ids.T, gate_fixed.T])
    x_parts, d_parts = spread(tokens, route, cotangent)
    me = lax.axis_index(PLANE).astype(jnp.int32).reshape(1)
    both, both_sent = [((2 * slots, hidden), t) for t in (F32, BF16)]
    place, scale, both, both_sent = call(
        "forward",
        functools.partial(route_body, wide, topk, block, capacity, len(x_parts)),
        [((total, slots), BF16), ((slots, LANES), F32), both, both_sent],
        [me] + x_parts + [w_gate, w_up],
        2 * product,
    )
    both_in = from_peers(both_sent)
    d_parts = spread_end(d_parts, [both_sent])
    sums = [((slots, hidden), F32), ((slots, hidden), BF16)]
    back, back_sent = call(
        "back", functools.partial(back_body, len(d_parts)), sums, d_parts + [place, w_down], product
    )
    back_in = from_peers(back_sent)
    placed = [((total // 2, features), F32)] + [((total // 4, features), BF16)] * 2
    near, got_first, got_second = collect_start(
        *call(
            "out",
            functools.partial(out_body, peers),
            placed,
            [both] + both_in + [scale, place, w_down, back_sent],
            product,
        )
    )
    half = near.shape[0] // 2
    (far,) = add(near, half, [(got_first, 0)], [(half, BF16)])
    factors = call(
        "factor",
        functools.partial(factor_body, peers),
        [((slots, hidden), F32)] * 2,
        [both] + both_in + [scale],
    )
    grad = collect_early(
        *collect_start(
            *call(
                "grad",
                functools.partial(grad_body, peers),
                placed,
                list(factors) + [back] + back_in + [place, w_gate, w_up, far],
                2 * product,
                24,
            )
        )
    )
    return collect_few(near, far, got_second), grad


def solution(mesh):
    rows = P(PLANE, "dp")
    placed = (
        rows,
        rows,
        P(PLANE, None),
        P(PLANE, None),
        P(PLANE, "dp", None),
        P(PLANE, "dp", None),
        P(PLANE, None, "dp"),
    )
    return jax.shard_map(
        on_device, mesh=mesh, in_specs=placed, out_specs=(rows, rows), check_vma=False
    )
```

```python
import functools

import jax
import jax.numpy as jnp
from jax import lax
from jax.experimental import pallas as pl
from jax.experimental.pallas import tpu as pltpu
from jax.sharding import PartitionSpec as P

PLANE = ("group", "ingroup")
LANES = 128
CHUNK = 256
PIECES = 4
BF16 = jnp.bfloat16
F32 = jnp.float32


def dot(left, right, left_dim=1, right_dim=0):
    return lax.dot_general(
        left, right, (((left_dim,), (right_dim,)), ((), ())), preferred_element_type=F32
    )


def call(name, body, outs, args, flops=0, limit=16, hbm=(), passed=(), scratch=(), weight=1):
    shapes = [jax.ShapeDtypeStruct(shape, dtype) for shape, dtype in outs]
    moved = sum(a.size * a.dtype.itemsize for a in args)
    moved += sum(s.size * s.dtype.itemsize for s in shapes)
    specs = [
        pl.BlockSpec(
            memory_space=pltpu.HBM if i in hbm else pltpu.SMEM if a.shape == (1,) else pltpu.VMEM
        )
        for i, a in enumerate(args)
    ]
    inputs, results = len(args), len(shapes)

    def run(*refs):
        ins, rest = refs[:inputs], refs[inputs + len(passed) :]
        body(*ins, *rest[:results], *rest[results + len(passed) :])

    free = pl.BlockSpec(memory_space=pl.ANY)
    kernel = pl.pallas_call(
        run,
        out_shape=shapes + [jax.ShapeDtypeStruct(p.shape, p.dtype) for p in passed],
        in_specs=specs + [free] * len(passed),
        out_specs=[pl.BlockSpec(memory_space=pltpu.VMEM)] * results + [free] * len(passed),
        input_output_aliases={inputs + i: results + i for i in range(len(passed))},
        scratch_shapes=list(scratch),
        compiler_params=pltpu.CompilerParams(vmem_limit_bytes=limit << 20),
        name=name,
        cost_estimate=pl.CostEstimate(flops=flops, bytes_accessed=moved * weight, transcendentals=0),
    )
    with jax.named_scope(name):
        return kernel(*args, *passed)


def swap(value, axis, offset):
    return lax.ppermute(value, axis, [(i, i ^ offset) for i in range(lax.axis_size(axis))])


def bits_of(axis):
    bits, bit = [], lax.axis_size(axis) // 2
    while bit:
        bits.append(bit)
        bit //= 2
    return bits


def routing_body(ids, gate, out):
    topk, block = ids.shape
    rows = jnp.concatenate(
        [
            ids[...].astype(F32),
            (gate[...] >> 8).astype(F32),
            (gate[...] & 255).astype(F32),
            jnp.zeros((LANES - 3 * topk, block), F32),
        ],
        axis=0,
    ).astype(BF16)
    eye = lax.broadcasted_iota(jnp.int32, (block, block), 0) == lax.broadcasted_iota(
        jnp.int32, (block, block), 1
    )
    out[...] = dot(jnp.where(eye, 1.0, 0.0).astype(BF16), rows, 1, 1).astype(BF16)


def merge_body(near_x, far_x, near_route, far_route, out):
    block, features = near_x.shape
    wide = out.shape[1] - LANES
    if wide != features:
        out[...] = jnp.zeros_like(out)
    out[:block, :features] = near_x[...]
    out[block:, :features] = far_x[...]
    out[:block, wide:] = near_route[...]
    out[block:, wide:] = far_route[...]


def pack_body(count, *refs):
    parts, out = refs[:count], refs[-1]
    at = 0
    for part in parts:
        out[at : at + part.shape[0]] = part[...]
        at += part.shape[0]


def pack(parts, after=()):
    shape = (sum(p.shape[0] for p in parts), parts[0].shape[1])
    return call(
        "pack",
        functools.partial(pack_body, len(parts)),
        [(shape, parts[0].dtype)],
        list(parts) + list(after),
        flops=1 << 29,
    )[0]


def copy_body(source, after, out):
    out[...] = source[...]


def copied(source, after):
    return call("copied", copy_body, [(source.shape, source.dtype)], [source, after], 1 << 31)[0]


def spread(tokens, route, cotangent):
    inner, outer = bits_of("ingroup"), bits_of("group")
    block, features = tokens.shape
    wide = -(-features // LANES) * LANES
    first, second = None, copied(cotangent, route)
    first, second = call(
        "merge",
        merge_body,
        [((2 * block, wide + LANES), BF16)],
        [tokens, swap(tokens, "ingroup", inner[0]), route, swap(route, "ingroup", inner[0])],
        passed=[second],
    )
    for bit in inner[1:-1]:
        first = pack([first, swap(first, "ingroup", bit)])
    beside = swap(first, "ingroup", inner[-1])
    across = swap(first, "group", outer[0])
    last = swap(beside, "group", outer[0])
    for bit in inner[:-1]:
        second = pack([second, swap(second, "ingroup", bit)])
    first = pack([first, beside, across, last], after=[second])
    beside = swap(second, "ingroup", inner[-1])
    for bit in outer[1:-1]:
        first = pack([first, swap(first, "group", bit)])
    first = [first, swap(first, "group", outer[-1])]
    return first, [second, beside]


def spread_end(parts, after):
    bits = bits_of("group")
    current = pack(parts, after)
    for bit in bits[:-1]:
        current = pack([current, swap(current, "group", bit)])
    return [current, swap(current, "group", bits[-1])]


def route_body(wide, topk, block, capacity, count, me, *refs):
    parts, rest = refs[:count], refs[count:]
    sources, (place_out, scale_out, part_out, sent_out, *held, sems) = rest[:2], rest[2:]
    features, hidden = sources[0].shape
    width = hidden // PIECES
    copies = []
    for i in range(2):
        for j in range(PIECES):
            piece = pl.ds(j * width, width)
            copy = pltpu.make_async_copy(
                sources[i].at[:, piece], held[i].at[:, piece], sems.at[i, j]
            )
            copy.start()
            copies.append(copy)
    total, slots = place_out.shape
    routing = jnp.concatenate([p[:, wide : wide + LANES] for p in parts], axis=0)
    lane = lax.broadcasted_iota(jnp.int32, (total, LANES), 1)
    match = (routing.astype(F32) == me[0].astype(F32)) & (lane < topk)
    source = lax.broadcasted_iota(jnp.int32, (LANES, LANES), 0)
    target = lax.broadcasted_iota(jnp.int32, (LANES, LANES), 1)

    def gate_half(offset):
        moved = dot(routing, jnp.where(source == target + offset, 1.0, 0.0).astype(BF16))
        own = jnp.where(match, moved, 0.0).astype(BF16)
        return dot(own, jnp.ones((LANES, LANES), BF16)).astype(BF16)

    named = dot(jnp.where(match, 1.0, 0.0).astype(BF16), jnp.ones((LANES, slots), BF16))
    chunk = min(total, CHUNK)
    row = lax.broadcasted_iota(jnp.int32, (chunk, chunk), 0)
    col = lax.broadcasted_iota(jnp.int32, (chunk, chunk), 1)
    earlier = jnp.where((row // block == col // block) & (row > col), 1.0, 0.0).astype(BF16)
    named_half = named.astype(BF16)
    rank = jnp.concatenate(
        [dot(earlier, named_half[i : i + chunk]) for i in range(0, total, chunk)], axis=0
    )
    start = lax.broadcasted_iota(jnp.int32, (total, slots), 0) // block * capacity
    slot = lax.broadcasted_iota(jnp.int32, (total, slots), 1) - start
    place = jnp.where((named > 0.5) & (rank == slot.astype(F32)), 1.0, 0.0).astype(BF16)
    place_out[...] = place
    high = dot(place, gate_half(topk), 0, 0)
    low = dot(place, gate_half(2 * topk), 0, 0)
    scale_out[...] = (high * 256.0 + low) / 65536.0
    values = jnp.concatenate([p[:, :features] for p in parts], axis=0)
    rows = dot(place, values, 0, 0).astype(BF16)
    for i in range(2):
        for j in range(PIECES):
            copies[i * PIECES + j].wait()
            columns = slice(j * width, (j + 1) * width)
            part = dot(rows, held[i][:, columns])
            part_out[i * slots : (i + 1) * slots, columns] = part
            sent_out[i * slots : (i + 1) * slots, columns] = part.astype(BF16)


def back_body(count, *refs):
    parts, (place, weight, part_out, sent_out) = refs[:count], refs[count:]
    values = jnp.concatenate([p[...] for p in parts], axis=0)
    rows = dot(place[...], values, 0, 0).astype(BF16)
    part = dot(rows, weight[...], 1, 1)
    part_out[...] = part
    sent_out[...] = part.astype(BF16)


def summed(own, received):
    total = own[...]
    for r in received:
        total = total + r[...].astype(F32)
    return total


def place_rows(place, rows, near_out, *far_outs):
    end = place.shape[0]
    for out in far_outs:
        start = end - out.shape[0]
        out[...] = dot(place[start:end], rows).astype(BF16)
        end = start
    near_out[...] = dot(place[:end], rows)


def forward_sums(both, received):
    total = summed(both, received)
    half = total.shape[0] // 2
    return total[:half], total[half:]


def out_body(peers, *refs):
    scale, place, weight, _, *outs = refs[1 + peers :]
    gate_pre, up_pre = forward_sums(refs[0], refs[1 : 1 + peers])
    hidden = (gate_pre / (1.0 + jnp.exp(-gate_pre)) * up_pre).astype(BF16)
    rows = (dot(hidden, weight[...]) * scale[:, :1]).astype(BF16)
    place_rows(place[...], rows, *outs)


def factor_body(peers, *refs):
    scale, gate_out, up_out = refs[1 + peers :]
    gate_pre, up_pre = forward_sums(refs[0], refs[1 : 1 + peers])
    sigmoid = 1.0 / (1.0 + jnp.exp(-gate_pre))
    scaled = sigmoid * scale[:, :1]
    gate_out[...] = up_pre * scaled * (1.0 + gate_pre * (1.0 - sigmoid))
    up_out[...] = gate_pre * scaled


def grad_body(peers, *refs):
    gate_factor, up_factor, back = refs[:3]
    back_in = refs[3 : 3 + peers]
    place, gate_weight, up_weight, _, *outs = refs[3 + peers :]
    d_hidden = summed(back, back_in)
    d_gate = (d_hidden * gate_factor[...]).astype(BF16)
    d_up = (d_hidden * up_factor[...]).astype(BF16)
    rows = (dot(d_gate, gate_weight[...], 1, 1) + dot(d_up, up_weight[...], 1, 1)).astype(BF16)
    place_rows(place[...], rows, *outs)


def add_body(count, at, parts, keep, *refs):
    rows = sum(out.shape[0] for out in refs[count:])
    total = keep[at : at + rows].astype(F32)
    for received, start in zip(refs[:count], parts):
        total = total + received[start : start + rows].astype(F32)
    start = 0
    for out in refs[count:]:
        out[...] = total[start : start + out.shape[0]].astype(out.dtype)
        start += out.shape[0]


def add(keep, at, received, outs):
    return call(
        "add",
        functools.partial(add_body, len(received), at, [start for _, start in received]),
        [((rows, keep.shape[1]), dtype) for rows, dtype in outs],
        [keep] + [r for r, _ in received],
    )


def collect_start(near, *pieces):
    for bit in reversed(bits_of("group")[2:]):
        half = near.shape[0] // 2
        got = jnp.concatenate([swap(piece, "group", bit) for piece in pieces[::-1]], axis=0)
        outs = [(piece.shape[0] // 2, BF16) for piece in pieces[::-1]]
        pieces = add(near, half, [(got, half)], outs)[::-1]
        (near,) = add(near, 0, [(got, 0)], [(half, F32)])
    return near, *[swap(piece, "group", bits_of("group")[1]) for piece in pieces]


def collect_end(near, far, bits):
    for bit in bits:
        received = swap(far, "ingroup", bit)
        half = near.shape[0] // 2
        if bit == bits[-1]:
            return add(near, 0, [(received, 0)], [(2 * half, BF16)])[0]
        near, far = add(near, 0, [(received, 0)], [(half, F32), (half, BF16)])


def collect_across(near, *got):
    half, bit = near.shape[0] // 2, bits_of("group")[0]
    quarter = half // 2
    if len(got) == 1:
        low, high = add(near, half, [(got[0], 0)], [(quarter, BF16)] * 2)
    else:
        (high,) = add(near, half + quarter, [(got[0], 0)], [(quarter, BF16)])
        (low,) = add(near, half, [(got[1], 0)], [(quarter, BF16)])
    return swap(high, "group", bit), swap(low, "group", bit)


def collect_rest(near, got_second, across, last):
    inner = bits_of("ingroup")
    half = near.shape[0] // 2
    quarter, eighth = half // 2, half // 4
    (far,) = add(near, quarter, [(got_second, quarter), (across, 0)], [(quarter, BF16)])
    beside = swap(far, "ingroup", inner[-1])
    near, far = add(
        near, 0, [(got_second, 0), (last, 0), (beside, 0)], [(eighth, F32), (eighth, BF16)]
    )
    return collect_end(near, far, inner[-2::-1])


def from_peers(sent):
    count = lax.axis_size("dp")
    return [
        lax.ppermute(sent, "dp", [(i, (i + step) % count) for i in range(count)])
        for step in range(1, count)
    ]


def on_device(tokens, cotangent, expert_ids, gate_fixed, w_gate, w_up, w_down):
    experts = lax.axis_size("group") * lax.axis_size("ingroup")
    block, features = tokens.shape
    topk = expert_ids.shape[1]
    hidden = w_gate.shape[2]
    capacity = 2 * block // lax.axis_size("ingroup")
    slots, total = experts * capacity, experts * block
    wide = -(-features // LANES) * LANES
    peers = lax.axis_size("dp") - 1
    w_gate, w_up, w_down = w_gate[0], w_up[0], w_down[0]
    product = 2 * slots * features * hidden

    (route,) = call("routing", routing_body, [((block, LANES), BF16)], [expert_ids.T, gate_fixed.T])
    x_parts, d_parts = spread(tokens, route, cotangent)
    me = lax.axis_index(PLANE).astype(jnp.int32).reshape(1)
    both, both_sent = [((2 * slots, hidden), t) for t in (F32, BF16)]
    place, scale, both, both_sent = call(
        "forward",
        functools.partial(route_body, wide, topk, block, capacity, len(x_parts)),
        [((total, slots), BF16), ((slots, LANES), F32), both, both_sent],
        [me] + x_parts + [w_gate, w_up],
        2 * product,
        50,
        hbm=(len(x_parts) + 1, len(x_parts) + 2),
        scratch=[pltpu.VMEM((features, hidden), BF16)] * 2
        + [pltpu.SemaphoreType.DMA((2, PIECES))],
    )
    both_in = from_peers(both_sent)
    d_parts = spread_end(d_parts, [both_sent])
    sums = [((slots, hidden), F32), ((slots, hidden), BF16)]
    back, back_sent = call(
        "back", functools.partial(back_body, len(d_parts)), sums, d_parts + [place, w_down], product
    )
    back_in = from_peers(back_sent)
    near = ((total // 2, features), F32)
    fourth, eighth = ((total // 4, features), BF16), ((total // 8, features), BF16)
    near_y, got_high, got_low, got_y = collect_start(
        *call(
            "out",
            functools.partial(out_body, peers),
            [near, eighth, eighth, fourth],
            [both] + both_in + [scale, place, w_down, back_sent],
            product,
        )
    )
    across, last = collect_across(near_y, got_high, got_low)
    factors = call(
        "factor",
        functools.partial(factor_body, peers),
        [((slots, hidden), F32)] * 2,
        [both] + both_in + [scale],
    )
    near_dx, got_first, got_dx = collect_start(
        *call(
            "grad",
            functools.partial(grad_body, peers),
            [near, fourth, fourth],
            list(factors) + [back] + back_in + [place, w_gate, w_up, across],
            2 * product,
            24,
        )
    )
    mixed = collect_rest(near_y, got_y, across, last)
    return mixed, collect_rest(near_dx, got_dx, *collect_across(near_dx, got_first))


def solution(mesh):
    rows = P(PLANE, "dp")
    placed = (
        rows,
        rows,
        P(PLANE, None),
        P(PLANE, None),
        P(PLANE, "dp", None),
        P(PLANE, "dp", None),
        P(PLANE, None, "dp"),
    )
    return jax.shard_map(
        on_device, mesh=mesh, in_specs=placed, out_specs=(rows, rows), check_vma=False
    )
```

```python
import functools

import jax
import jax.numpy as jnp
from jax import lax
from jax.experimental import pallas as pl
from jax.experimental.pallas import tpu as pltpu
from jax.sharding import PartitionSpec as P

PLANE = ("group", "ingroup")
LANES = 128
CHUNK = 256
FETCH = 50
BF16 = jnp.bfloat16
F32 = jnp.float32


def dot(left, right, left_dim=1, right_dim=0):
    return lax.dot_general(
        left, right, (((left_dim,), (right_dim,)), ((), ())), preferred_element_type=F32
    )


def call(name, body, outs, args, flops=0, limit=16, hbm=(), passed=(), scratch=(), weight=1):
    shapes = [jax.ShapeDtypeStruct(shape, dtype) for shape, dtype in outs]
    moved = sum(a.size * a.dtype.itemsize for a in args)
    moved += sum(s.size * s.dtype.itemsize for s in shapes)
    specs = [
        pl.BlockSpec(
            memory_space=pltpu.HBM if i in hbm else pltpu.SMEM if a.shape == (1,) else pltpu.VMEM
        )
        for i, a in enumerate(args)
    ]
    inputs, results = len(args), len(shapes)

    def run(*refs):
        ins, rest = refs[:inputs], refs[inputs + len(passed) :]
        body(*ins, *rest[:results], *rest[results + len(passed) :])

    free = pl.BlockSpec(memory_space=pl.ANY)
    kernel = pl.pallas_call(
        run,
        out_shape=shapes + [jax.ShapeDtypeStruct(p.shape, p.dtype) for p in passed],
        in_specs=specs + [free] * len(passed),
        out_specs=[pl.BlockSpec(memory_space=pltpu.VMEM)] * results + [free] * len(passed),
        input_output_aliases={inputs + i: results + i for i in range(len(passed))},
        scratch_shapes=list(scratch),
        compiler_params=pltpu.CompilerParams(vmem_limit_bytes=limit << 20),
        name=name,
        cost_estimate=pl.CostEstimate(flops=flops, bytes_accessed=moved * weight, transcendentals=0),
    )
    with jax.named_scope(name):
        return kernel(*args, *passed)


def swap(value, axis, offset):
    return lax.ppermute(value, axis, [(i, i ^ offset) for i in range(lax.axis_size(axis))])


def bits_of(axis):
    bits, bit = [], lax.axis_size(axis) // 2
    while bit:
        bits.append(bit)
        bit //= 2
    return bits


def payload_body(tokens, ids, gate, out, tokens_held, ids_held, gate_held, sems):
    copies = [
        pltpu.make_async_copy(source, held, sems.at[i])
        for i, (source, held) in enumerate(
            ((ids, ids_held), (gate, gate_held), (tokens, tokens_held))
        )
    ]
    for copy in copies:
        copy.start()
    topk, block = ids.shape
    features = tokens.shape[1]
    wide = out.shape[1] - LANES
    if wide != features:
        out[...] = jnp.zeros_like(out)
    eye = lax.broadcasted_iota(jnp.int32, (block, block), 0) == lax.broadcasted_iota(
        jnp.int32, (block, block), 1
    )
    copies[0].wait()
    copies[1].wait()
    rows = jnp.concatenate(
        [
            ids_held[...].astype(F32),
            (gate_held[...] >> 8).astype(F32),
            (gate_held[...] & 255).astype(F32),
            jnp.zeros((LANES - 3 * topk, block), F32),
        ],
        axis=0,
    ).astype(BF16)
    out[:, wide:] = dot(jnp.where(eye, 1.0, 0.0).astype(BF16), rows, 1, 1).astype(BF16)
    copies[2].wait()
    out[:, :features] = tokens_held[...]


def fetch_body(source, after, out, token, sem):
    copy = pltpu.make_async_copy(source, out, sem)
    copy.start()
    token[...] = jnp.zeros_like(token)
    copy.wait()


def fetch(source, after):
    return call(
        "fetch",
        fetch_body,
        [(source.shape, source.dtype), ((8, LANES), F32)],
        [source, after],
        limit=FETCH,
        hbm=(0,),
        scratch=[pltpu.SemaphoreType.DMA],
    )


def pack_body(count, *refs):
    parts, out = refs[:count], refs[-1]
    at = 0
    for part in parts:
        out[at : at + part.shape[0]] = part[...]
        at += part.shape[0]


def pack(parts, after=(), passed=()):
    shape = (sum(p.shape[0] for p in parts), parts[0].shape[1])
    out = call(
        "pack",
        functools.partial(pack_body, len(parts)),
        [(shape, parts[0].dtype)],
        list(parts) + list(after),
        flops=1 << 29,
        passed=passed,
    )
    return out if passed else out[0]


def copy_body(source, after, out):
    out[...] = source[...]


def copied(source, after):
    return call("copied", copy_body, [(source.shape, source.dtype)], [source, after], 1 << 31)[0]


def spread(own, cotangent, w_gate, w_up):
    outer, inner_count = bits_of("group"), lax.axis_size("ingroup")
    second = copied(cotangent, own)
    blocks = [own] + [swap(own, "ingroup", j) for j in range(1, inner_count)]
    w_gate, token = fetch(w_gate, own)
    early = pack(blocks[: inner_count // 2], [token])
    w_up, token = fetch(w_up, early)
    late, second = pack(blocks[inner_count // 2 :], passed=[second])
    across = swap(early, "group", outer[0])
    last = swap(late, "group", outer[0])
    *bits, high = bits_of("ingroup")[::-1]
    for bit in bits:
        second = pack([second, swap(second, "ingroup", bit)])
    first = pack([early, late, across, last], [token, second])
    for bit in outer[1:-1]:
        first = pack([first, swap(first, "group", bit)])
    first = [first, swap(first, "group", outer[-1])]
    return first, [second, swap(second, "ingroup", high)], w_gate, w_up


def spread_end(parts, after):
    bits = bits_of("group")
    current = pack(parts, after)
    for bit in bits[:-1]:
        current = pack([current, swap(current, "group", bit)])
    return [current, swap(current, "group", bits[-1])]


def route_body(wide, topk, block, capacity, count, me, *refs):
    parts, (gate_weight, up_weight, place_out, scale_out, part_out, sent_out) = (
        refs[:count],
        refs[count:],
    )
    features = gate_weight.shape[0]
    total, slots = place_out.shape
    routing = jnp.concatenate([p[:, wide : wide + LANES] for p in parts], axis=0)
    lane = lax.broadcasted_iota(jnp.int32, (total, LANES), 1)
    match = (routing.astype(F32) == me[0].astype(F32)) & (lane < topk)
    source = lax.broadcasted_iota(jnp.int32, (LANES, LANES), 0)
    target = lax.broadcasted_iota(jnp.int32, (LANES, LANES), 1)

    def gate_half(offset):
        moved = dot(routing, jnp.where(source == target + offset, 1.0, 0.0).astype(BF16))
        own = jnp.where(match, moved, 0.0).astype(BF16)
        return dot(own, jnp.ones((LANES, LANES), BF16)).astype(BF16)

    named = dot(jnp.where(match, 1.0, 0.0).astype(BF16), jnp.ones((LANES, slots), BF16))
    chunk = min(total, CHUNK)
    row = lax.broadcasted_iota(jnp.int32, (chunk, chunk), 0)
    col = lax.broadcasted_iota(jnp.int32, (chunk, chunk), 1)
    earlier = jnp.where((row // block == col // block) & (row > col), 1.0, 0.0).astype(BF16)
    named_half = named.astype(BF16)
    rank = jnp.concatenate(
        [dot(earlier, named_half[i : i + chunk]) for i in range(0, total, chunk)], axis=0
    )
    start = lax.broadcasted_iota(jnp.int32, (total, slots), 0) // block * capacity
    slot = lax.broadcasted_iota(jnp.int32, (total, slots), 1) - start
    place = jnp.where((named > 0.5) & (rank == slot.astype(F32)), 1.0, 0.0).astype(BF16)
    place_out[...] = place
    high = dot(place, gate_half(topk), 0, 0)
    low = dot(place, gate_half(2 * topk), 0, 0)
    scale_out[...] = (high * 256.0 + low) / 65536.0
    values = jnp.concatenate([p[:, :features] for p in parts], axis=0)
    rows = dot(place, values, 0, 0).astype(BF16)
    for i, weight in enumerate((gate_weight, up_weight)):
        part = dot(rows, weight[...])
        part_out[i * slots : (i + 1) * slots] = part
        sent_out[i * slots : (i + 1) * slots] = part.astype(BF16)


def back_body(count, *refs):
    parts, (place, weight, part_out, sent_out) = refs[:count], refs[count:]
    values = jnp.concatenate([p[...] for p in parts], axis=0)
    rows = dot(place[...], values, 0, 0).astype(BF16)
    part = dot(rows, weight[...], 1, 1)
    part_out[...] = part
    sent_out[...] = part.astype(BF16)


def summed(own, received):
    total = own[...]
    for r in received:
        total = total + r[...].astype(F32)
    return total


def place_rows(place, rows, near_out, *far_outs):
    end = place.shape[0]
    for out in far_outs:
        start = end - out.shape[0]
        out[...] = dot(place[start:end], rows).astype(BF16)
        end = start
    near_out[...] = dot(place[:end], rows)


def forward_sums(both, received):
    total = summed(both, received)
    half = total.shape[0] // 2
    return total[:half], total[half:]


def out_body(peers, *refs):
    scale, place, weight, _, *outs = refs[1 + peers :]
    gate_pre, up_pre = forward_sums(refs[0], refs[1 : 1 + peers])
    hidden = (gate_pre / (1.0 + jnp.exp(-gate_pre)) * up_pre).astype(BF16)
    rows = (dot(hidden, weight[...]) * scale[:, :1]).astype(BF16)
    place_rows(place[...], rows, *outs)


def factor_body(peers, *refs):
    scale, gate_out, up_out = refs[1 + peers :]
    gate_pre, up_pre = forward_sums(refs[0], refs[1 : 1 + peers])
    sigmoid = 1.0 / (1.0 + jnp.exp(-gate_pre))
    scaled = sigmoid * scale[:, :1]
    gate_out[...] = up_pre * scaled * (1.0 + gate_pre * (1.0 - sigmoid))
    up_out[...] = gate_pre * scaled


def grad_body(peers, *refs):
    gate_factor, up_factor, back = refs[:3]
    back_in = refs[3 : 3 + peers]
    place, gate_weight, up_weight, _, *outs = refs[3 + peers :]
    d_hidden = summed(back, back_in)
    d_gate = (d_hidden * gate_factor[...]).astype(BF16)
    d_up = (d_hidden * up_factor[...]).astype(BF16)
    rows = (dot(d_gate, gate_weight[...], 1, 1) + dot(d_up, up_weight[...], 1, 1)).astype(BF16)
    place_rows(place[...], rows, *outs)


def add_body(count, at, parts, keep, *refs):
    rows = sum(out.shape[0] for out in refs[count:])
    total = keep[at : at + rows].astype(F32)
    for received, start in zip(refs[:count], parts):
        total = total + received[start : start + rows].astype(F32)
    start = 0
    for out in refs[count:]:
        out[...] = total[start : start + out.shape[0]].astype(out.dtype)
        start += out.shape[0]


def add(keep, at, received, outs):
    return call(
        "add",
        functools.partial(add_body, len(received), at, [start for _, start in received]),
        [((rows, keep.shape[1]), dtype) for rows, dtype in outs],
        [keep] + [r for r, _ in received],
    )


def collect_start(near, *pieces):
    for bit in reversed(bits_of("group")[2:]):
        half = near.shape[0] // 2
        got = jnp.concatenate([swap(piece, "group", bit) for piece in pieces[::-1]], axis=0)
        outs = [(piece.shape[0] // 2, BF16) for piece in pieces[::-1]]
        pieces = add(near, half, [(got, half)], outs)[::-1]
        (near,) = add(near, 0, [(got, 0)], [(half, F32)])
    return near, *[swap(piece, "group", bits_of("group")[1]) for piece in pieces]


def collect_few(near, far, got_stay):
    half = near.shape[0] // 2
    received = [(got_stay, 0), (swap(far, "group", bits_of("group")[0]), 0)]
    for bit in bits_of("ingroup"):
        half //= 2
        near, far = add(near, 0, received, [(half, F32), (half, BF16)])
        received = [(swap(far, "ingroup", bit), 0)]
    return add(near, 0, received, [(half, BF16)])[0]


def collect_soon(near, got_go, got_stay):
    count, bit = lax.axis_size("ingroup"), bits_of("group")[0]
    half = near.shape[0] // 2
    quarter, block = half // 2, half // count
    low, high = add(near, half, [(got_go, 0)], [(quarter, BF16)] * 2)
    across, last = swap(high, "group", bit), swap(low, "group", bit)
    away = add(near, quarter, [(got_stay, quarter), (across, 0)], [(block, BF16)] * (count // 2))
    sent = [swap(away[j], "ingroup", count // 2 + j) for j in range(count // 2)[::-1]]
    own, *away = add(
        near, 0, [(got_stay, 0), (last, 0)], [(block, F32)] + [(block, BF16)] * (count // 2 - 1)
    )
    sent += [swap(away[j], "ingroup", 1 + j) for j in range(count // 2 - 1)[::-1]]
    return add(own, 0, [(s, 0) for s in sent], [(block, BF16)])[0]


def from_peers(sent):
    count = lax.axis_size("dp")
    return [
        lax.ppermute(sent, "dp", [(i, (i + step) % count) for i in range(count)])
        for step in range(1, count)
    ]


def on_device(tokens, cotangent, expert_ids, gate_fixed, w_gate, w_up, w_down):
    experts = lax.axis_size("group") * lax.axis_size("ingroup")
    block, features = tokens.shape
    topk = expert_ids.shape[1]
    hidden = w_gate.shape[2]
    capacity = 2 * block // lax.axis_size("ingroup")
    slots, total = experts * capacity, experts * block
    wide = -(-features // LANES) * LANES
    peers = lax.axis_size("dp") - 1
    w_gate, w_up, w_down = w_gate[0], w_up[0], w_down[0]
    product = 2 * slots * features * hidden

    (own,) = call(
        "payload",
        payload_body,
        [((block, wide + LANES), BF16)],
        [tokens, expert_ids.T, gate_fixed.T],
        limit=58,
        hbm=(0, 1, 2),
        scratch=[pltpu.VMEM(tokens.shape, BF16)]
        + [pltpu.VMEM((topk, block), jnp.int32)] * 2
        + [pltpu.SemaphoreType.DMA((3,))],
    )
    x_parts, d_parts, gate_held, up_held = spread(own, cotangent, w_gate, w_up)
    me = lax.axis_index(PLANE).astype(jnp.int32).reshape(1)
    both, both_sent = [((2 * slots, hidden), t) for t in (F32, BF16)]
    place, scale, both, both_sent = call(
        "forward",
        functools.partial(route_body, wide, topk, block, capacity, len(x_parts)),
        [((total, slots), BF16), ((slots, LANES), F32), both, both_sent],
        [me] + x_parts + [gate_held, up_held],
        2 * product,
        16,
    )
    both_in = from_peers(both_sent)
    d_parts = spread_end(d_parts, [both_sent])
    sums = [((slots, hidden), F32), ((slots, hidden), BF16)]
    back, back_sent = call(
        "back", functools.partial(back_body, len(d_parts)), sums, d_parts + [place, w_down], product
    )
    back_in = from_peers(back_sent)
    near = ((total // 2, features), F32)
    fourth = ((total // 4, features), BF16)
    near_y, got_go, got_y = collect_start(
        *call(
            "out",
            functools.partial(out_body, peers),
            [near, fourth, fourth],
            [both] + both_in + [scale, place, w_down, back_sent],
            product,
        )
    )
    (far,) = add(near_y, near_y.shape[0] // 2, [(got_go, 0)], [(near_y.shape[0] // 2, BF16)])
    factors = call(
        "factor",
        functools.partial(factor_body, peers),
        [((slots, hidden), F32)] * 2,
        [both] + both_in + [scale],
    )
    near_dx, got_go, got_dx = collect_start(
        *call(
            "grad",
            functools.partial(grad_body, peers),
            [near, fourth, fourth],
            list(factors) + [back] + back_in + [place, gate_held, up_held, far],
            2 * product,
            24,
        )
    )
    return collect_few(near_y, far, got_y), collect_soon(near_dx, got_go, got_dx)


def solution(mesh):
    rows = P(PLANE, "dp")
    placed = (
        rows,
        rows,
        P(PLANE, None),
        P(PLANE, None),
        P(PLANE, "dp", None),
        P(PLANE, "dp", None),
        P(PLANE, None, "dp"),
    )
    return jax.shard_map(
        on_device, mesh=mesh, in_specs=placed, out_specs=(rows, rows), check_vma=False
    )
```

```python
import functools

import jax
import jax.numpy as jnp
from jax import lax
from jax.experimental import pallas as pl
from jax.experimental.pallas import tpu as pltpu
from jax.sharding import PartitionSpec as P

PLANE = ("group", "ingroup")
LANES = 128
CHUNK = 256
BF16 = jnp.bfloat16
F32 = jnp.float32


def dot(left, right, left_dim=1, right_dim=0):
    return lax.dot_general(
        left, right, (((left_dim,), (right_dim,)), ((), ())), preferred_element_type=F32
    )


def call(name, body, outs, args, flops=0, limit=16, hbm=(), passed=(), scratch=(), weight=1):
    shapes = [jax.ShapeDtypeStruct(shape, dtype) for shape, dtype in outs]
    moved = sum(a.size * a.dtype.itemsize for a in args)
    moved += sum(s.size * s.dtype.itemsize for s in shapes)
    specs = [
        pl.BlockSpec(
            memory_space=pltpu.HBM if i in hbm else pltpu.SMEM if a.shape == (1,) else pltpu.VMEM
        )
        for i, a in enumerate(args)
    ]
    inputs, results = len(args), len(shapes)

    def run(*refs):
        ins, rest = refs[:inputs], refs[inputs + len(passed) :]
        body(*ins, *rest[:results], *rest[results + len(passed) :])

    free = pl.BlockSpec(memory_space=pl.ANY)
    kernel = pl.pallas_call(
        run,
        out_shape=shapes + [jax.ShapeDtypeStruct(p.shape, p.dtype) for p in passed],
        in_specs=specs + [free] * len(passed),
        out_specs=[pl.BlockSpec(memory_space=pltpu.VMEM)] * results + [free] * len(passed),
        input_output_aliases={inputs + i: results + i for i in range(len(passed))},
        scratch_shapes=list(scratch),
        compiler_params=pltpu.CompilerParams(vmem_limit_bytes=limit << 20),
        name=name,
        cost_estimate=pl.CostEstimate(flops=flops, bytes_accessed=moved * weight, transcendentals=0),
    )
    with jax.named_scope(name):
        return kernel(*args, *passed)


def swap(value, axis, offset):
    return lax.ppermute(value, axis, [(i, i ^ offset) for i in range(lax.axis_size(axis))])


def bits_of(axis):
    bits, bit = [], lax.axis_size(axis) // 2
    while bit:
        bits.append(bit)
        bit //= 2
    return bits


def payload_body(me, tokens, ids, gate, out, tokens_held, ids_held, gate_held, sems):
    copies = [
        pltpu.make_async_copy(source, held, sems.at[i])
        for i, (source, held) in enumerate(
            ((ids, ids_held), (gate, gate_held), (tokens, tokens_held))
        )
    ]
    for copy in copies:
        copy.start()
    topk, block = ids.shape
    features = tokens.shape[1]
    wide = out.shape[1] - LANES
    if wide != features:
        out[...] = jnp.zeros_like(out)
    eye = lax.broadcasted_iota(jnp.int32, (block, block), 0) == lax.broadcasted_iota(
        jnp.int32, (block, block), 1
    )
    copies[0].wait()
    copies[1].wait()
    rows = jnp.concatenate(
        [
            ids_held[...].astype(F32),
            (gate_held[...] >> 8).astype(F32),
            (gate_held[...] & 255).astype(F32),
            jnp.zeros((LANES - 3 * topk, block), F32),
        ],
        axis=0,
    ).astype(BF16)
    out[:, wide:] = dot(jnp.where(eye, 1.0, 0.0).astype(BF16), rows, 1, 1).astype(BF16)
    copies[2].wait()
    out[:, :features] = tokens_held[...]


def pack_body(count, *refs):
    parts, out = refs[:count], refs[-1]
    at = 0
    for part in parts:
        out[at : at + part.shape[0]] = part[...]
        at += part.shape[0]


def pack(parts, after=(), passed=()):
    shape = (sum(p.shape[0] for p in parts), parts[0].shape[1])
    out = call(
        "pack",
        functools.partial(pack_body, len(parts)),
        [(shape, parts[0].dtype)],
        list(parts) + list(after),
        flops=1 << 29,
        passed=passed,
    )
    return out if passed else out[0]


def copy_body(source, after, out):
    out[...] = source[...]


def copied(source, after):
    return call("copied", copy_body, [(source.shape, source.dtype)], [source, after], 1 << 31)[0]


def exchange(own):
    count = lax.axis_size("ingroup")
    return [own] + [swap(own, "ingroup", j) for j in range(1, count)]


def spread(own, cotangent):
    outer = bits_of("group")
    blocks = exchange(own)
    half = len(blocks) // 2
    early, second = pack(blocks[:half], passed=[copied(cotangent, own)])
    second = exchange(second)
    late = pack(blocks[half:])
    across = swap(early, "group", outer[0])
    last = swap(late, "group", outer[0])
    first = pack([early, late, across, last], second)
    for bit in outer[1:-1]:
        first = pack([first, swap(first, "group", bit)])
    return [first, swap(first, "group", outer[-1])], second


def spread_end(parts, after):
    bits = bits_of("group")
    current = pack(parts, after)
    for bit in bits[:-1]:
        current = pack([current, swap(current, "group", bit)])
    return [current, swap(current, "group", bits[-1])]


def route_body(wide, topk, block, capacity, count, me, *refs):
    parts, (gate_weight, up_weight, place_out, scale_out, part_out, sent_out) = (
        refs[:count],
        refs[count:],
    )
    features = gate_weight.shape[0]
    total, slots = place_out.shape
    routing = jnp.concatenate([p[:, wide : wide + LANES] for p in parts], axis=0)
    lane = lax.broadcasted_iota(jnp.int32, (total, LANES), 1)
    match = (routing.astype(F32) == me[0].astype(F32)) & (lane < topk)
    source = lax.broadcasted_iota(jnp.int32, (LANES, LANES), 0)
    target = lax.broadcasted_iota(jnp.int32, (LANES, LANES), 1)

    def gate_half(offset):
        moved = dot(routing, jnp.where(source == target + offset, 1.0, 0.0).astype(BF16))
        own = jnp.where(match, moved, 0.0).astype(BF16)
        return dot(own, jnp.ones((LANES, LANES), BF16)).astype(BF16)

    named = dot(jnp.where(match, 1.0, 0.0).astype(BF16), jnp.ones((LANES, slots), BF16))
    chunk = min(total, CHUNK)
    row = lax.broadcasted_iota(jnp.int32, (chunk, chunk), 0)
    col = lax.broadcasted_iota(jnp.int32, (chunk, chunk), 1)
    earlier = jnp.where((row // block == col // block) & (row > col), 1.0, 0.0).astype(BF16)
    named_half = named.astype(BF16)
    rank = jnp.concatenate(
        [dot(earlier, named_half[i : i + chunk]) for i in range(0, total, chunk)], axis=0
    )
    start = lax.broadcasted_iota(jnp.int32, (total, slots), 0) // block * capacity
    slot = lax.broadcasted_iota(jnp.int32, (total, slots), 1) - start
    place = jnp.where((named > 0.5) & (rank == slot.astype(F32)), 1.0, 0.0).astype(BF16)
    place_out[...] = place
    high = dot(place, gate_half(topk), 0, 0)
    low = dot(place, gate_half(2 * topk), 0, 0)
    scale_out[...] = (high * 256.0 + low) / 65536.0
    values = jnp.concatenate([p[:, :features] for p in parts], axis=0)
    rows = dot(place, values, 0, 0).astype(BF16)
    for i, weight in enumerate((gate_weight, up_weight)):
        part = dot(rows, weight[...])
        part_out[i * slots : (i + 1) * slots] = part
        sent_out[i * slots : (i + 1) * slots] = part.astype(BF16)


def back_body(count, *refs):
    parts, (place, weight, part_out, sent_out) = refs[:count], refs[count:]
    values = jnp.concatenate([p[...] for p in parts], axis=0)
    rows = dot(place[...], values, 0, 0).astype(BF16)
    part = dot(rows, weight[...], 1, 1)
    part_out[...] = part
    sent_out[...] = part.astype(BF16)


def summed(own, received):
    total = own[...]
    for r in received:
        total = total + r[...].astype(F32)
    return total


def place_rows(place, rows, near_out, *far_outs):
    end = place.shape[0]
    for out in far_outs:
        start = end - out.shape[0]
        out[...] = dot(place[start:end], rows).astype(BF16)
        end = start
    near_out[...] = dot(place[:end], rows)


def forward_sums(both, received):
    total = summed(both, received)
    half = total.shape[0] // 2
    return total[:half], total[half:]


def out_body(peers, *refs):
    scale, place, weight, _, *outs = refs[1 + peers :]
    gate_pre, up_pre = forward_sums(refs[0], refs[1 : 1 + peers])
    hidden = (gate_pre / (1.0 + jnp.exp(-gate_pre)) * up_pre).astype(BF16)
    rows = (dot(hidden, weight[...]) * scale[:, :1]).astype(BF16)
    place_rows(place[...], rows, *outs)


def factor_body(peers, *refs):
    scale, gate_out, up_out = refs[1 + peers :]
    gate_pre, up_pre = forward_sums(refs[0], refs[1 : 1 + peers])
    sigmoid = 1.0 / (1.0 + jnp.exp(-gate_pre))
    scaled = sigmoid * scale[:, :1]
    gate_out[...] = up_pre * scaled * (1.0 + gate_pre * (1.0 - sigmoid))
    up_out[...] = gate_pre * scaled


def grad_body(peers, *refs):
    gate_factor, up_factor, back = refs[:3]
    back_in = refs[3 : 3 + peers]
    place, gate_weight, up_weight, _, *outs = refs[3 + peers :]
    d_hidden = summed(back, back_in)
    d_gate = (d_hidden * gate_factor[...]).astype(BF16)
    d_up = (d_hidden * up_factor[...]).astype(BF16)
    rows = (dot(d_gate, gate_weight[...], 1, 1) + dot(d_up, up_weight[...], 1, 1)).astype(BF16)
    place_rows(place[...], rows, *outs)


def add_body(count, after, at, parts, keep, *refs):
    outs = refs[count + after :]
    rows = sum(out.shape[0] for out in outs)
    total = keep[at : at + rows].astype(F32)
    for received, start in zip(refs[:count], parts):
        total = total + received[start : start + rows].astype(F32)
    start = 0
    for out in outs:
        out[...] = total[start : start + out.shape[0]].astype(out.dtype)
        start += out.shape[0]


def add(keep, at, received, outs, after=()):
    return call(
        "add",
        functools.partial(
            add_body, len(received), len(after), at, [start for _, start in received]
        ),
        [((rows, keep.shape[1]), dtype) for rows, dtype in outs],
        [keep] + [r for r, _ in received] + list(after),
    )


def collect_start(near, *pieces):
    for bit in reversed(bits_of("group")[2:]):
        half = near.shape[0] // 2
        got = jnp.concatenate([swap(piece, "group", bit) for piece in pieces[::-1]], axis=0)
        outs = [(piece.shape[0] // 2, BF16) for piece in pieces[::-1]]
        pieces = add(near, half, [(got, half)], outs)[::-1]
        (near,) = add(near, 0, [(got, 0)], [(half, F32)])
    return near, *[swap(piece, "group", bits_of("group")[1]) for piece in pieces]


def collect_few(near, far, got_stay, ties):
    half = near.shape[0] // 2
    received = [(got_stay, 0), (swap(far, "group", bits_of("group")[0]), 0)]
    for i, bit in enumerate(bits_of("ingroup")):
        half //= 2
        near, far = add(near, 0, received, [(half, F32), (half, BF16)], ties[i : i + 1])
        received = [(swap(far, "ingroup", bit), 0)]
    return add(near, 0, received, [(half, BF16)])[0]


def collect_soon(near, got_go, got_stay):
    count, bit = lax.axis_size("ingroup"), bits_of("group")[0]
    half = near.shape[0] // 2
    quarter, block = half // 2, half // count
    low, high = add(near, half, [(got_go, 0)], [(quarter, BF16)] * 2)
    across, last = swap(high, "group", bit), swap(low, "group", bit)
    away = add(near, quarter, [(got_stay, quarter), (across, 0)], [(block, BF16)] * (count // 2))
    sent = [swap(away[j], "ingroup", count // 2 + j) for j in range(count // 2)[::-1]]
    outs = [(block, F32)] + [(block, BF16)] * (count // 2 - 1)
    own, *away = add(near, 0, [(got_stay, 0), (last, 0)], outs, away[:1])
    sent += [swap(away[j], "ingroup", 1 + j) for j in range(count // 2 - 1)[::-1]]
    return add(own, 0, [(s, 0) for s in sent], [(block, BF16)])[0], [low, own]


def from_peers(sent):
    count = lax.axis_size("dp")
    return [
        lax.ppermute(sent, "dp", [(i, (i + step) % count) for i in range(count)])
        for step in range(1, count)
    ]


def on_device(tokens, cotangent, expert_ids, gate_fixed, w_gate, w_up, w_down):
    experts = lax.axis_size("group") * lax.axis_size("ingroup")
    block, features = tokens.shape
    topk = expert_ids.shape[1]
    hidden = w_gate.shape[2]
    capacity = 2 * block // lax.axis_size("ingroup")
    slots, total = experts * capacity, experts * block
    wide = -(-features // LANES) * LANES
    peers = lax.axis_size("dp") - 1
    w_gate, w_up, w_down = w_gate[0], w_up[0], w_down[0]
    product = 2 * slots * features * hidden

    me = lax.axis_index(PLANE).astype(jnp.int32).reshape(1)
    (own,) = call(
        "payload",
        payload_body,
        [((block, wide + LANES), BF16)],
        [me, tokens, expert_ids.T, gate_fixed.T],
        limit=58,
        hbm=(1, 2, 3),
        scratch=[pltpu.VMEM(tokens.shape, BF16)]
        + [pltpu.VMEM((topk, block), jnp.int32)] * 2
        + [pltpu.SemaphoreType.DMA((3,))],
    )
    x_parts, d_parts = spread(own, cotangent)
    both, both_sent = [((2 * slots, hidden), t) for t in (F32, BF16)]
    place, scale, both, both_sent = call(
        "forward",
        functools.partial(route_body, wide, topk, block, capacity, len(x_parts)),
        [((total, slots), BF16), ((slots, LANES), F32), both, both_sent],
        [me] + x_parts + [w_gate, w_up],
        2 * product,
        16,
    )
    both_in = from_peers(both_sent)
    d_parts = spread_end(d_parts, [both_sent])
    sums = [((slots, hidden), F32), ((slots, hidden), BF16)]
    back, back_sent = call(
        "back", functools.partial(back_body, len(d_parts)), sums, d_parts + [place, w_down], product
    )
    back_in = from_peers(back_sent)
    near = ((total // 2, features), F32)
    fourth = ((total // 4, features), BF16)
    near_y, got_go, got_y = collect_start(
        *call(
            "out",
            functools.partial(out_body, peers),
            [near, fourth, fourth],
            [both] + both_in + [scale, place, w_down, back_sent],
            product,
        )
    )
    (far,) = add(near_y, near_y.shape[0] // 2, [(got_go, 0)], [(near_y.shape[0] // 2, BF16)])
    factors = call(
        "factor",
        functools.partial(factor_body, peers),
        [((slots, hidden), F32)] * 2,
        [both] + both_in + [scale],
    )
    near_dx, got_go, got_dx = collect_start(
        *call(
            "grad",
            functools.partial(grad_body, peers),
            [near, fourth, fourth],
            list(factors) + [back] + back_in + [place, w_gate, w_up, far],
            2 * product,
            24,
        )
    )
    grad, ties = collect_soon(near_dx, got_go, got_dx)
    return collect_few(near_y, far, got_y, ties), grad


def solution(mesh):
    rows = P(PLANE, "dp")
    placed = (
        rows,
        rows,
        P(PLANE, None),
        P(PLANE, None),
        P(PLANE, "dp", None),
        P(PLANE, "dp", None),
        P(PLANE, None, "dp"),
    )
    return jax.shard_map(
        on_device, mesh=mesh, in_specs=placed, out_specs=(rows, rows), check_vma=False
    )
```

```python
import functools

import jax
import jax.numpy as jnp
from jax import lax
from jax.experimental import pallas as pl
from jax.experimental.pallas import tpu as pltpu
from jax.sharding import PartitionSpec as P

PLANE = ("group", "ingroup")
LANES = 128
CHUNK = 256
BF16 = jnp.bfloat16
F32 = jnp.float32


def dot(left, right, left_dim=1, right_dim=0):
    return lax.dot_general(
        left, right, (((left_dim,), (right_dim,)), ((), ())), preferred_element_type=F32
    )


def call(name, body, outs, args, flops=0, limit=16, hbm=(), passed=(), scratch=(), weight=1):
    shapes = [jax.ShapeDtypeStruct(shape, dtype) for shape, dtype in outs]
    moved = sum(a.size * a.dtype.itemsize for a in args)
    moved += sum(s.size * s.dtype.itemsize for s in shapes)
    specs = [
        pl.BlockSpec(
            memory_space=pltpu.HBM if i in hbm else pltpu.SMEM if a.shape == (1,) else pltpu.VMEM
        )
        for i, a in enumerate(args)
    ]
    inputs, results = len(args), len(shapes)

    def run(*refs):
        ins, rest = refs[:inputs], refs[inputs + len(passed) :]
        body(*ins, *rest[:results], *rest[results + len(passed) :])

    free = pl.BlockSpec(memory_space=pl.ANY)
    kernel = pl.pallas_call(
        run,
        out_shape=shapes + [jax.ShapeDtypeStruct(p.shape, p.dtype) for p in passed],
        in_specs=specs + [free] * len(passed),
        out_specs=[pl.BlockSpec(memory_space=pltpu.VMEM)] * results + [free] * len(passed),
        input_output_aliases={inputs + i: results + i for i in range(len(passed))},
        scratch_shapes=list(scratch),
        compiler_params=pltpu.CompilerParams(vmem_limit_bytes=limit << 20),
        name=name,
        cost_estimate=pl.CostEstimate(flops=flops, bytes_accessed=moved * weight, transcendentals=0),
    )
    with jax.named_scope(name):
        return kernel(*args, *passed)


def swap(value, axis, offset):
    return lax.ppermute(value, axis, [(i, i ^ offset) for i in range(lax.axis_size(axis))])


def bits_of(axis):
    bits, bit = [], lax.axis_size(axis) // 2
    while bit:
        bits.append(bit)
        bit //= 2
    return bits


def payload_body(me, tokens, ids, gate, out, tokens_held, ids_held, gate_held, sems):
    copies = [
        pltpu.make_async_copy(source, held, sems.at[i])
        for i, (source, held) in enumerate(
            ((ids, ids_held), (gate, gate_held), (tokens, tokens_held))
        )
    ]
    for copy in copies:
        copy.start()
    topk, block = ids.shape
    features = tokens.shape[1]
    wide = out.shape[1] - LANES
    if wide != features:
        out[...] = jnp.zeros_like(out)
    eye = lax.broadcasted_iota(jnp.int32, (block, block), 0) == lax.broadcasted_iota(
        jnp.int32, (block, block), 1
    )
    copies[0].wait()
    copies[1].wait()
    rows = jnp.concatenate(
        [
            ids_held[...].astype(F32),
            (gate_held[...] >> 8).astype(F32),
            (gate_held[...] & 255).astype(F32),
            jnp.zeros((LANES - 3 * topk, block), F32),
        ],
        axis=0,
    ).astype(BF16)
    out[:, wide:] = dot(jnp.where(eye, 1.0, 0.0).astype(BF16), rows, 1, 1).astype(BF16)
    copies[2].wait()
    out[:, :features] = tokens_held[...]


def pack_body(count, *refs):
    parts, out = refs[:count], refs[-1]
    at = 0
    for part in parts:
        out[at : at + part.shape[0]] = part[...]
        at += part.shape[0]


def pack(parts, after=(), passed=()):
    shape = (sum(p.shape[0] for p in parts), parts[0].shape[1])
    out = call(
        "pack",
        functools.partial(pack_body, len(parts)),
        [(shape, parts[0].dtype)],
        list(parts) + list(after),
        flops=1 << 29,
        passed=passed,
    )
    return out if passed else out[0]


def copy_body(source, after, out):
    out[...] = source[...]


def copied(source, after):
    return call("copied", copy_body, [(source.shape, source.dtype)], [source, after], 1 << 31)[0]


def spread(own, cotangent):
    outer, count = bits_of("group"), lax.axis_size("ingroup")
    blocks = [own] + [swap(own, "ingroup", j) for j in range(1, count)]
    early, second = pack(blocks[: count // 2], passed=[copied(cotangent, own)])
    late = pack(blocks[count // 2 :])
    across = swap(early, "group", outer[0])
    last = swap(late, "group", outer[0])
    for bit in bits_of("ingroup")[:0:-1]:
        second = pack([second, swap(second, "ingroup", bit)])
    first = pack([early, late, across, last], [second])
    for bit in outer[1:-1]:
        first = pack([first, swap(first, "group", bit)])
    first = [first, swap(first, "group", outer[-1])]
    return first, [second, swap(second, "ingroup", bits_of("ingroup")[0])]


def spread_end(parts, after):
    bits = bits_of("group")
    current = pack(parts, after)
    for bit in bits[:-1]:
        current = pack([current, swap(current, "group", bit)])
    return [current, swap(current, "group", bits[-1])]


def route_body(wide, topk, block, capacity, count, me, *refs):
    parts, (gate_weight, up_weight, place_out, scale_out, part_out, sent_out) = (
        refs[:count],
        refs[count:],
    )
    features = gate_weight.shape[0]
    total, slots = place_out.shape
    routing = jnp.concatenate([p[:, wide : wide + LANES] for p in parts], axis=0)
    lane = lax.broadcasted_iota(jnp.int32, (total, LANES), 1)
    match = (routing.astype(F32) == me[0].astype(F32)) & (lane < topk)
    source = lax.broadcasted_iota(jnp.int32, (LANES, LANES), 0)
    target = lax.broadcasted_iota(jnp.int32, (LANES, LANES), 1)

    def gate_half(offset):
        moved = dot(routing, jnp.where(source == target + offset, 1.0, 0.0).astype(BF16))
        own = jnp.where(match, moved, 0.0).astype(BF16)
        return dot(own, jnp.ones((LANES, LANES), BF16)).astype(BF16)

    named = dot(jnp.where(match, 1.0, 0.0).astype(BF16), jnp.ones((LANES, slots), BF16))
    chunk = min(total, CHUNK)
    row = lax.broadcasted_iota(jnp.int32, (chunk, chunk), 0)
    col = lax.broadcasted_iota(jnp.int32, (chunk, chunk), 1)
    earlier = jnp.where((row // block == col // block) & (row > col), 1.0, 0.0).astype(BF16)
    named_half = named.astype(BF16)
    rank = jnp.concatenate(
        [dot(earlier, named_half[i : i + chunk]) for i in range(0, total, chunk)], axis=0
    )
    start = lax.broadcasted_iota(jnp.int32, (total, slots), 0) // block * capacity
    slot = lax.broadcasted_iota(jnp.int32, (total, slots), 1) - start
    place = jnp.where((named > 0.5) & (rank == slot.astype(F32)), 1.0, 0.0).astype(BF16)
    place_out[...] = place
    high = dot(place, gate_half(topk), 0, 0)
    low = dot(place, gate_half(2 * topk), 0, 0)
    scale_out[...] = (high * 256.0 + low) / 65536.0
    values = jnp.concatenate([p[:, :features] for p in parts], axis=0)
    rows = dot(place, values, 0, 0).astype(BF16)
    for i, weight in enumerate((gate_weight, up_weight)):
        part = dot(rows, weight[...])
        part_out[i * slots : (i + 1) * slots] = part
        sent_out[i * slots : (i + 1) * slots] = part.astype(BF16)


def back_body(count, *refs):
    parts, (place, weight, part_out, sent_out) = refs[:count], refs[count:]
    values = jnp.concatenate([p[...] for p in parts], axis=0)
    rows = dot(place[...], values, 0, 0).astype(BF16)
    part = dot(rows, weight[...], 1, 1)
    part_out[...] = part
    sent_out[...] = part.astype(BF16)


def summed(own, received):
    total = own[...]
    for r in received:
        total = total + r[...].astype(F32)
    return total


def place_rows(place, rows, near_out, *far_outs):
    end = place.shape[0]
    for out in far_outs:
        start = end - out.shape[0]
        out[...] = dot(place[start:end], rows).astype(BF16)
        end = start
    near_out[...] = dot(place[:end], rows)


def forward_sums(both, received):
    total = summed(both, received)
    half = total.shape[0] // 2
    return total[:half], total[half:]


def out_body(peers, *refs):
    scale, place, weight, _, gate_out, up_out, *outs = refs[1 + peers :]
    gate_pre, up_pre = forward_sums(refs[0], refs[1 : 1 + peers])
    sigmoid = 1.0 / (1.0 + jnp.exp(-gate_pre))
    silu = gate_pre * sigmoid
    rows = (dot((silu * up_pre).astype(BF16), weight[...]) * scale[:, :1]).astype(BF16)
    place_rows(place[...], rows, *outs)
    scaled = sigmoid * scale[:, :1]
    gate_out[...] = up_pre * scaled * (1.0 + gate_pre * (1.0 - sigmoid))
    up_out[...] = silu * scale[:, :1]


def grad_body(peers, *refs):
    gate_factor, up_factor, back = refs[:3]
    gate_weight, up_weight, _, rows_out = refs[3 + peers :]
    d_hidden = summed(back, refs[3 : 3 + peers])
    d_gate = (d_hidden * gate_factor[...]).astype(BF16)
    d_up = (d_hidden * up_factor[...]).astype(BF16)
    rows_out[...] = (
        dot(d_gate, gate_weight[...], 1, 1) + dot(d_up, up_weight[...], 1, 1)
    ).astype(BF16)


def place_body(place, rows, keep, stay, received, near_out, go_out, stay_out, keep_out, far_out):
    place_rows(place[...], rows[...], near_out, go_out, stay_out)
    half = keep_out.shape[0]
    total = keep[: 2 * half] + stay[...].astype(F32) + received[...].astype(F32)
    keep_out[...] = total[:half]
    far_out[...] = total[half:].astype(BF16)


def join_body(near, stay, last, keep, got, own_out, mixed_out, pair_out, *away_outs):
    block = own_out.shape[0]
    rows = last.shape[0]
    total = near[:rows] + stay[:rows].astype(F32) + last[...].astype(F32)
    mixed = keep[...] + got[...].astype(F32)
    own_out[...] = total[:block]
    mixed_out[...] = mixed[:block]
    pair_out[:block] = mixed[block:].astype(BF16)
    pair_out[block:] = total[block : 2 * block].astype(BF16)
    for i, out in enumerate(away_outs):
        out[...] = total[(2 + i) * block : (3 + i) * block].astype(BF16)


def final_body(count, mixed, grad, pair, *refs):
    block = mixed.shape[0]
    mixed_out, grad_out = refs[count:]
    mixed_out[...] = (mixed[...] + pair[:block].astype(F32)).astype(BF16)
    grad_out[...] = (summed(grad, refs[:count]) + pair[block:].astype(F32)).astype(BF16)


def add_body(count, after, at, parts, keep, *refs):
    outs = refs[count + after :]
    rows = sum(out.shape[0] for out in outs)
    total = keep[at : at + rows].astype(F32)
    for received, start in zip(refs[:count], parts):
        total = total + received[start : start + rows].astype(F32)
    start = 0
    for out in outs:
        out[...] = total[start : start + out.shape[0]].astype(out.dtype)
        start += out.shape[0]


def far_body(keep, low, high, out):
    half = out.shape[0]
    middle = low.shape[0]
    out[:middle] = (keep[half : half + middle] + low[...].astype(F32)).astype(BF16)
    out[middle:] = (keep[half + middle :] + high[...].astype(F32)).astype(BF16)


def add(keep, at, received, outs, after=()):
    return call(
        "add",
        functools.partial(
            add_body, len(received), len(after), at, [start for _, start in received]
        ),
        [((rows, keep.shape[1]), dtype) for rows, dtype in outs],
        [keep] + [r for r, _ in received] + list(after),
    )


def collect_start(near, *pieces):
    for bit in reversed(bits_of("group")[2:]):
        half = near.shape[0] // 2
        got = jnp.concatenate([swap(piece, "group", bit) for piece in pieces[::-1]], axis=0)
        outs = [(piece.shape[0] // 2, BF16) for piece in pieces[::-1]]
        pieces = add(near, half, [(got, half)], outs)[::-1]
        (near,) = add(near, 0, [(got, 0)], [(half, F32)])
    return near, *[swap(piece, "group", bits_of("group")[1]) for piece in pieces]


def from_peers(sent):
    count = lax.axis_size("dp")
    return [
        lax.ppermute(sent, "dp", [(i, (i + step) % count) for i in range(count)])
        for step in range(1, count)
    ]


def on_device(tokens, cotangent, expert_ids, gate_fixed, w_gate, w_up, w_down):
    experts = lax.axis_size("group") * lax.axis_size("ingroup")
    block, features = tokens.shape
    topk = expert_ids.shape[1]
    hidden = w_gate.shape[2]
    capacity = 2 * block // lax.axis_size("ingroup")
    slots, total = experts * capacity, experts * block
    wide = -(-features // LANES) * LANES
    peers = lax.axis_size("dp") - 1
    w_gate, w_up, w_down = w_gate[0], w_up[0], w_down[0]
    product = 2 * slots * features * hidden

    me = lax.axis_index(PLANE).astype(jnp.int32).reshape(1)
    (own,) = call(
        "payload",
        payload_body,
        [((block, wide + LANES), BF16)],
        [me, tokens, expert_ids.T, gate_fixed.T],
        limit=58,
        hbm=(1, 2, 3),
        scratch=[pltpu.VMEM(tokens.shape, BF16)]
        + [pltpu.VMEM((topk, block), jnp.int32)] * 2
        + [pltpu.SemaphoreType.DMA((3,))],
    )
    x_parts, d_parts = spread(own, cotangent)
    both, both_sent = [((2 * slots, hidden), t) for t in (F32, BF16)]
    place, scale, both, both_sent = call(
        "forward",
        functools.partial(route_body, wide, topk, block, capacity, len(x_parts)),
        [((total, slots), BF16), ((slots, LANES), F32), both, both_sent],
        [me] + x_parts + [w_gate, w_up],
        2 * product,
        16,
    )
    both_in = from_peers(both_sent)
    d_parts = spread_end(d_parts, [both_sent])
    sums = [((slots, hidden), F32), ((slots, hidden), BF16)]
    back, back_sent = call(
        "back", functools.partial(back_body, len(d_parts)), sums, d_parts + [place, w_down], product
    )
    back_in = from_peers(back_sent)
    near = ((total // 2, features), F32)
    fourth, eighth = ((total // 4, features), BF16), ((total // 8, features), BF16)
    gate_factor, up_factor, *placed = call(
        "out",
        functools.partial(out_body, peers),
        [((slots, hidden), F32)] * 2 + [near, eighth, eighth, fourth],
        [both] + both_in + [scale, place, w_down, back_sent],
        product,
    )
    near_y, got_high, got_low, got_y = collect_start(*placed)
    half = near_y.shape[0] // 2
    (far,) = call(
        "add",
        far_body,
        [((half, features), BF16)],
        [near_y, got_low, got_high],
    )
    (rows,) = call(
        "grad",
        functools.partial(grad_body, peers),
        [((slots, features), BF16)],
        [gate_factor, up_factor, back] + back_in + [w_gate, w_up, far],
        2 * product,
        24,
    )
    axis, bits = "ingroup", bits_of("ingroup")
    count, across_bit = lax.axis_size("ingroup"), bits_of("group")[0]
    near_dx, go, stay, keep, far = call(
        "place",
        place_body,
        [near, fourth, fourth] + [((half // 2, features), t) for t in (F32, BF16)],
        [place, rows, near_y, got_y, swap(far, "group", across_bit)],
    )
    near_dx, got_go, got_dx = collect_start(near_dx, go, stay)
    got = swap(far, axis, bits[0])
    for bit in bits[1:-1]:
        outs = [(keep.shape[0] // 2, t) for t in (F32, BF16)]
        keep, far = add(keep, 0, [(got, 0)], outs)
        got = swap(far, axis, bit)
    (far,) = add(near_dx, half, [(got_go, 0)], [(half, BF16)])
    own_dx, own_y, pair, *away = call(
        "join",
        join_body,
        [((block, features), F32)] * 2
        + [((2 * block, features), BF16)]
        + [((block, features), BF16)] * (count - 2),
        [near_dx, got_dx, swap(far, "group", across_bit), keep, got],
    )
    sent = [swap(part, axis, 2 + j) for j, part in enumerate(away)]
    outs = [((block, features), BF16)] * 2
    return call(
        "final",
        functools.partial(final_body, len(sent)),
        outs,
        [own_y, own_dx, swap(pair, axis, 1)] + sent,
    )


def solution(mesh):
    rows = P(PLANE, "dp")
    placed = (
        rows,
        rows,
        P(PLANE, None),
        P(PLANE, None),
        P(PLANE, "dp", None),
        P(PLANE, "dp", None),
        P(PLANE, None, "dp"),
    )
    return jax.shard_map(
        on_device, mesh=mesh, in_specs=placed, out_specs=(rows, rows), check_vma=False
    )
```

```python
import functools

import jax
import jax.numpy as jnp
from jax import lax
from jax.experimental import pallas as pl
from jax.experimental.pallas import tpu as pltpu
from jax.sharding import PartitionSpec as P

PLANE = ("group", "ingroup")
LANES = 128
CHUNK = 256
BF16 = jnp.bfloat16
F32 = jnp.float32


def dot(left, right, left_dim=1, right_dim=0):
    return lax.dot_general(
        left, right, (((left_dim,), (right_dim,)), ((), ())), preferred_element_type=F32
    )


def call(name, body, outs, args, flops=0, limit=16, hbm=(), passed=(), scratch=(), weight=1):
    shapes = [jax.ShapeDtypeStruct(shape, dtype) for shape, dtype in outs]
    moved = sum(a.size * a.dtype.itemsize for a in args)
    moved += sum(s.size * s.dtype.itemsize for s in shapes)
    specs = [
        pl.BlockSpec(
            memory_space=pltpu.HBM if i in hbm else pltpu.SMEM if a.shape == (1,) else pltpu.VMEM
        )
        for i, a in enumerate(args)
    ]
    inputs, results = len(args), len(shapes)

    def run(*refs):
        ins, rest = refs[:inputs], refs[inputs + len(passed) :]
        body(*ins, *rest[:results], *rest[results + len(passed) :])

    free = pl.BlockSpec(memory_space=pl.ANY)
    kernel = pl.pallas_call(
        run,
        out_shape=shapes + [jax.ShapeDtypeStruct(p.shape, p.dtype) for p in passed],
        in_specs=specs + [free] * len(passed),
        out_specs=[pl.BlockSpec(memory_space=pltpu.VMEM)] * results + [free] * len(passed),
        input_output_aliases={inputs + i: results + i for i in range(len(passed))},
        scratch_shapes=list(scratch),
        compiler_params=pltpu.CompilerParams(vmem_limit_bytes=limit << 20),
        name=name,
        cost_estimate=pl.CostEstimate(flops=flops, bytes_accessed=moved * weight, transcendentals=0),
    )
    with jax.named_scope(name):
        return kernel(*args, *passed)


def swap(value, axis, offset):
    return lax.ppermute(value, axis, [(i, i ^ offset) for i in range(lax.axis_size(axis))])


def bits_of(axis):
    bits, bit = [], lax.axis_size(axis) // 2
    while bit:
        bits.append(bit)
        bit //= 2
    return bits


def payload_body(me, tokens, ids, gate, out, tokens_held, ids_held, gate_held, sems):
    copies = [
        pltpu.make_async_copy(source, held, sems.at[i])
        for i, (source, held) in enumerate(
            ((ids, ids_held), (gate, gate_held), (tokens, tokens_held))
        )
    ]
    for copy in copies:
        copy.start()
    topk, block = ids.shape
    features = tokens.shape[1]
    wide = out.shape[1] - LANES
    if wide != features:
        out[...] = jnp.zeros_like(out)
    eye = lax.broadcasted_iota(jnp.int32, (block, block), 0) == lax.broadcasted_iota(
        jnp.int32, (block, block), 1
    )
    copies[0].wait()
    copies[1].wait()
    rows = jnp.concatenate(
        [
            ids_held[...].astype(F32),
            (gate_held[...] >> 8).astype(F32),
            (gate_held[...] & 255).astype(F32),
            jnp.zeros((LANES - 3 * topk, block), F32),
        ],
        axis=0,
    ).astype(BF16)
    out[:, wide:] = dot(jnp.where(eye, 1.0, 0.0).astype(BF16), rows, 1, 1).astype(BF16)
    copies[2].wait()
    out[:, :features] = tokens_held[...]


def pack_body(count, *refs):
    parts, out = refs[:count], refs[-1]
    at = 0
    for part in parts:
        out[at : at + part.shape[0]] = part[...]
        at += part.shape[0]


def pack(parts, after=(), passed=()):
    shape = (sum(p.shape[0] for p in parts), parts[0].shape[1])
    out = call(
        "pack",
        functools.partial(pack_body, len(parts)),
        [(shape, parts[0].dtype)],
        list(parts) + list(after),
        flops=1 << 29,
        passed=passed,
    )
    return out if passed else out[0]


def copy_body(source, after, out):
    out[...] = source[...]


def copied(source, after):
    return call("copied", copy_body, [(source.shape, source.dtype)], [source, after], 1 << 31)[0]


def inner_order():
    bits = bits_of("ingroup")
    return [
        sum(bit for i, bit in enumerate(bits) if k >> i & 1)
        for k in range(lax.axis_size("ingroup"))
    ]


def spread(own, cotangent):
    outer, inner = bits_of("group"), bits_of("ingroup")
    blocks = [own] + [swap(own, "ingroup", j) for j in inner_order()[1:]]
    half = len(blocks) // 2
    second = copied(cotangent, blocks[half])
    early = pack(blocks[:half])
    for bit in inner[:-1]:
        second = pack([second, swap(second, "ingroup", bit)])
    late = pack(blocks[half:], [early])
    across = swap(early, "group", outer[0])
    last = swap(late, "group", outer[0])
    first = pack([early, late, across, last], [second])
    for bit in outer[1:-1]:
        first = pack([first, swap(first, "group", bit)])
    first = [first, swap(first, "group", outer[-1])]
    return first, [second, swap(second, "ingroup", inner[-1])]


def spread_end(parts, after):
    held = [pack(parts, after)]
    for bit in bits_of("group"):
        held = held + [swap(part, "group", bit) for part in held]
    return held


def route_body(wide, topk, block, capacity, count, me, *refs):
    parts, (gate_weight, up_weight, place_out, scale_out, part_out, sent_out) = (
        refs[:count],
        refs[count:],
    )
    features = gate_weight.shape[0]
    total, slots = place_out.shape
    routing = jnp.concatenate([p[:, wide : wide + LANES] for p in parts], axis=0)
    lane = lax.broadcasted_iota(jnp.int32, (total, LANES), 1)
    match = (routing.astype(F32) == me[0].astype(F32)) & (lane < topk)
    source = lax.broadcasted_iota(jnp.int32, (LANES, LANES), 0)
    target = lax.broadcasted_iota(jnp.int32, (LANES, LANES), 1)

    def gate_half(offset):
        moved = dot(routing, jnp.where(source == target + offset, 1.0, 0.0).astype(BF16))
        own = jnp.where(match, moved, 0.0).astype(BF16)
        return dot(own, jnp.ones((LANES, LANES), BF16)).astype(BF16)

    named = dot(jnp.where(match, 1.0, 0.0).astype(BF16), jnp.ones((LANES, slots), BF16))
    chunk = min(total, CHUNK)
    row = lax.broadcasted_iota(jnp.int32, (chunk, chunk), 0)
    col = lax.broadcasted_iota(jnp.int32, (chunk, chunk), 1)
    earlier = jnp.where((row // block == col // block) & (row > col), 1.0, 0.0).astype(BF16)
    named_half = named.astype(BF16)
    rank = jnp.concatenate(
        [dot(earlier, named_half[i : i + chunk]) for i in range(0, total, chunk)], axis=0
    )
    start = lax.broadcasted_iota(jnp.int32, (total, slots), 0) // block * capacity
    slot = lax.broadcasted_iota(jnp.int32, (total, slots), 1) - start
    place = jnp.where((named > 0.5) & (rank == slot.astype(F32)), 1.0, 0.0).astype(BF16)
    place_out[...] = place
    high = dot(place, gate_half(topk), 0, 0)
    low = dot(place, gate_half(2 * topk), 0, 0)
    scale_out[...] = (high * 256.0 + low) / 65536.0
    values = jnp.concatenate([p[:, :features] for p in parts], axis=0)
    rows = dot(place, values, 0, 0).astype(BF16)
    for i, weight in enumerate((gate_weight, up_weight)):
        part = dot(rows, weight[...])
        part_out[i * slots : (i + 1) * slots] = part
        sent_out[i * slots : (i + 1) * slots] = part.astype(BF16)


def back_body(count, *refs):
    parts, (place, weight, part_out, sent_out) = refs[:count], refs[count:]
    values = jnp.concatenate([p[...] for p in parts], axis=0)
    rows = dot(place[...], values, 0, 0).astype(BF16)
    part = dot(rows, weight[...], 1, 1)
    part_out[...] = part
    sent_out[...] = part.astype(BF16)


def summed(own, received):
    total = own[...]
    for r in received:
        total = total + r[...].astype(F32)
    return total


def place_rows(place, rows, near_out, *far_outs):
    end = place.shape[0]
    for out in far_outs:
        start = end - out.shape[0]
        out[...] = dot(place[start:end], rows).astype(BF16)
        end = start
    near_out[...] = dot(place[:end], rows)


def forward_sums(both, received):
    total = summed(both, received)
    half = total.shape[0] // 2
    return total[:half], total[half:]


def out_body(peers, *refs):
    scale, place, weight, _, gate_out, up_out, *outs = refs[1 + peers :]
    gate_pre, up_pre = forward_sums(refs[0], refs[1 : 1 + peers])
    sigmoid = 1.0 / (1.0 + jnp.exp(-gate_pre))
    silu = gate_pre * sigmoid
    rows = (dot((silu * up_pre).astype(BF16), weight[...]) * scale[:, :1]).astype(BF16)
    place_rows(place[...], rows, *outs)
    scaled = sigmoid * scale[:, :1]
    gate_out[...] = up_pre * scaled * (1.0 + gate_pre * (1.0 - sigmoid))
    up_out[...] = silu * scale[:, :1]


def grad_body(peers, *refs):
    gate_factor, up_factor, back = refs[:3]
    gate_weight, up_weight, _, rows_out = refs[3 + peers :]
    d_hidden = summed(back, refs[3 : 3 + peers])
    d_gate = (d_hidden * gate_factor[...]).astype(BF16)
    d_up = (d_hidden * up_factor[...]).astype(BF16)
    rows_out[...] = (
        dot(d_gate, gate_weight[...], 1, 1) + dot(d_up, up_weight[...], 1, 1)
    ).astype(BF16)


def place_body(
    block, place, rows, keep, stay, received, near_out, go_out, stay_out, keep_out, far_out
):
    place_rows(place[...], rows[...], near_out, go_out, stay_out)
    half = keep_out.shape[0]
    total = keep[: 2 * half] + stay[...].astype(F32) + received[...].astype(F32)
    for at in range(0, half, block):
        keep_out[at : at + block] = total[2 * at : 2 * at + block]
        far_out[at : at + block] = total[2 * at + block : 2 * (at + block)].astype(BF16)


def join_body(near, stay, last, keep, got, own_out, mixed_out, pair_out, *away_outs):
    block = own_out.shape[0]
    rows = last.shape[0]
    total = near[:rows] + stay[:rows].astype(F32) + last[...].astype(F32)
    mixed = keep[...] + got[...].astype(F32)
    middle = rows // 2
    own_out[...] = total[:block]
    mixed_out[...] = mixed[:block]
    pair_out[:block] = mixed[block:].astype(BF16)
    pair_out[block:] = total[middle : middle + block].astype(BF16)
    starts = [at for at in range(block, rows, block) if at != middle]
    for at, out in zip(starts, away_outs):
        out[...] = total[at : at + block].astype(BF16)


def final_body(count, mixed, grad, pair, *refs):
    block = mixed.shape[0]
    mixed_out, grad_out = refs[count:]
    mixed_out[...] = (mixed[...] + pair[:block].astype(F32)).astype(BF16)
    grad_out[...] = (summed(grad, refs[:count]) + pair[block:].astype(F32)).astype(BF16)


def add_body(count, after, at, parts, keep, *refs):
    outs = refs[count + after :]
    rows = sum(out.shape[0] for out in outs)
    total = keep[at : at + rows].astype(F32)
    for received, start in zip(refs[:count], parts):
        total = total + received[start : start + rows].astype(F32)
    start = 0
    for out in outs:
        out[...] = total[start : start + out.shape[0]].astype(out.dtype)
        start += out.shape[0]


def far_body(keep, low, high, out):
    half = out.shape[0]
    middle = low.shape[0]
    out[:middle] = (keep[half : half + middle] + low[...].astype(F32)).astype(BF16)
    out[middle:] = (keep[half + middle :] + high[...].astype(F32)).astype(BF16)


def add(keep, at, received, outs, after=()):
    return call(
        "add",
        functools.partial(
            add_body, len(received), len(after), at, [start for _, start in received]
        ),
        [((rows, keep.shape[1]), dtype) for rows, dtype in outs],
        [keep] + [r for r, _ in received] + list(after),
    )


def collect_start(near, *pieces):
    for bit in reversed(bits_of("group")[2:]):
        half = near.shape[0] // 2
        got = jnp.concatenate([swap(piece, "group", bit) for piece in pieces[::-1]], axis=0)
        outs = [(piece.shape[0] // 2, BF16) for piece in pieces[::-1]]
        pieces = add(near, half, [(got, half)], outs)[::-1]
        (near,) = add(near, 0, [(got, 0)], [(half, F32)])
    return near, *[swap(piece, "group", bits_of("group")[1]) for piece in pieces]


def from_peers(sent):
    count = lax.axis_size("dp")
    return [
        lax.ppermute(sent, "dp", [(i, (i + step) % count) for i in range(count)])
        for step in range(1, count)
    ]


def on_device(tokens, cotangent, expert_ids, gate_fixed, w_gate, w_up, w_down):
    experts = lax.axis_size("group") * lax.axis_size("ingroup")
    block, features = tokens.shape
    topk = expert_ids.shape[1]
    hidden = w_gate.shape[2]
    capacity = 2 * block // lax.axis_size("ingroup")
    slots, total = experts * capacity, experts * block
    wide = -(-features // LANES) * LANES
    peers = lax.axis_size("dp") - 1
    w_gate, w_up, w_down = w_gate[0], w_up[0], w_down[0]
    product = 2 * slots * features * hidden

    me = lax.axis_index(PLANE).astype(jnp.int32).reshape(1)
    (own,) = call(
        "payload",
        payload_body,
        [((block, wide + LANES), BF16)],
        [me, tokens, expert_ids.T, gate_fixed.T],
        limit=58,
        hbm=(1, 2, 3),
        scratch=[pltpu.VMEM(tokens.shape, BF16)]
        + [pltpu.VMEM((topk, block), jnp.int32)] * 2
        + [pltpu.SemaphoreType.DMA((3,))],
    )
    x_parts, d_parts = spread(own, cotangent)
    both, both_sent = [((2 * slots, hidden), t) for t in (F32, BF16)]
    place, scale, both, both_sent = call(
        "forward",
        functools.partial(route_body, wide, topk, block, capacity, len(x_parts)),
        [((total, slots), BF16), ((slots, LANES), F32), both, both_sent],
        [me] + x_parts + [w_gate, w_up],
        2 * product,
        16,
    )
    both_in = from_peers(both_sent)
    d_parts = spread_end(d_parts, [both_sent])
    sums = [((slots, hidden), F32), ((slots, hidden), BF16)]
    back, back_sent = call(
        "back", functools.partial(back_body, len(d_parts)), sums, d_parts + [place, w_down], product
    )
    back_in = from_peers(back_sent)
    near = ((total // 2, features), F32)
    fourth, eighth = ((total // 4, features), BF16), ((total // 8, features), BF16)
    gate_factor, up_factor, *placed = call(
        "out",
        functools.partial(out_body, peers),
        [((slots, hidden), F32)] * 2 + [near, eighth, eighth, fourth],
        [both] + both_in + [scale, place, w_down, back_sent],
        product,
    )
    near_y, got_high, got_low, got_y = collect_start(*placed)
    half = near_y.shape[0] // 2
    (far,) = call(
        "add",
        far_body,
        [((half, features), BF16)],
        [near_y, got_low, got_high],
    )
    (rows,) = call(
        "grad",
        functools.partial(grad_body, peers),
        [((slots, features), BF16)],
        [gate_factor, up_factor, back] + back_in + [w_gate, w_up, far],
        2 * product,
        24,
    )
    axis, bits = "ingroup", bits_of("ingroup")
    count, across_bit = lax.axis_size("ingroup"), bits_of("group")[0]
    near_dx, go, stay, keep, far = call(
        "place",
        functools.partial(place_body, block),
        [near, fourth, fourth] + [((half // 2, features), t) for t in (F32, BF16)],
        [place, rows, near_y, got_y, swap(far, "group", across_bit)],
    )
    near_dx, got_go, got_dx = collect_start(near_dx, go, stay)
    got = swap(far, axis, bits[0])
    for bit in bits[1:-1]:
        sums = (keep + got.astype(F32)).reshape(-1, 2, block, features)
        keep = sums[:, 0].reshape(-1, features)
        got = swap(sums[:, 1].reshape(-1, features).astype(BF16), axis, bit)
    (far,) = add(near_dx, half, [(got_go, 0)], [(half, BF16)])
    own_dx, own_y, pair, *away = call(
        "join",
        join_body,
        [((block, features), F32)] * 2
        + [((2 * block, features), BF16)]
        + [((block, features), BF16)] * (count - 2),
        [near_dx, got_dx, swap(far, "group", across_bit), keep, got],
    )
    offsets = [j for j in inner_order() if j > 1]
    sent = [swap(part, axis, j) for j, part in zip(offsets, away)]
    outs = [((block, features), BF16)] * 2
    return call(
        "final",
        functools.partial(final_body, len(sent)),
        outs,
        [own_y, own_dx, swap(pair, axis, 1)] + sent,
    )


def solution(mesh):
    rows = P(PLANE, "dp")
    placed = (
        rows,
        rows,
        P(PLANE, None),
        P(PLANE, None),
        P(PLANE, "dp", None),
        P(PLANE, "dp", None),
        P(PLANE, None, "dp"),
    )
    return jax.shard_map(
        on_device, mesh=mesh, in_specs=placed, out_specs=(rows, rows), check_vma=False
    )
```

```python
import functools

import jax
import jax.numpy as jnp
from jax import lax
from jax.experimental import pallas as pl
from jax.experimental.pallas import tpu as pltpu
from jax.sharding import PartitionSpec as P

PLANE = ("group", "ingroup")
LANES = 128
CHUNK = 256
BF16 = jnp.bfloat16
F32 = jnp.float32


def dot(left, right, left_dim=1, right_dim=0):
    return lax.dot_general(
        left, right, (((left_dim,), (right_dim,)), ((), ())), preferred_element_type=F32
    )


def call(name, body, outs, args, flops=0, limit=16, hbm=(), passed=(), scratch=(), weight=1):
    shapes = [jax.ShapeDtypeStruct(shape, dtype) for shape, dtype in outs]
    moved = sum(a.size * a.dtype.itemsize for a in args)
    moved += sum(s.size * s.dtype.itemsize for s in shapes)
    specs = [
        pl.BlockSpec(
            memory_space=pltpu.HBM if i in hbm else pltpu.SMEM if a.shape == (1,) else pltpu.VMEM
        )
        for i, a in enumerate(args)
    ]
    inputs, results = len(args), len(shapes)

    def run(*refs):
        ins, rest = refs[:inputs], refs[inputs + len(passed) :]
        body(*ins, *rest[:results], *rest[results + len(passed) :])

    free = pl.BlockSpec(memory_space=pl.ANY)
    kernel = pl.pallas_call(
        run,
        out_shape=shapes + [jax.ShapeDtypeStruct(p.shape, p.dtype) for p in passed],
        in_specs=specs + [free] * len(passed),
        out_specs=[pl.BlockSpec(memory_space=pltpu.VMEM)] * results + [free] * len(passed),
        input_output_aliases={inputs + i: results + i for i in range(len(passed))},
        scratch_shapes=list(scratch),
        compiler_params=pltpu.CompilerParams(vmem_limit_bytes=limit << 20),
        name=name,
        cost_estimate=pl.CostEstimate(flops=flops, bytes_accessed=moved * weight, transcendentals=0),
    )
    with jax.named_scope(name):
        return kernel(*args, *passed)


def swap(value, axis, offset):
    return lax.ppermute(value, axis, [(i, i ^ offset) for i in range(lax.axis_size(axis))])


def bits_of(axis):
    bits, bit = [], lax.axis_size(axis) // 2
    while bit:
        bits.append(bit)
        bit //= 2
    return bits


def payload_body(me, tokens, ids, gate, out, tokens_held, ids_held, gate_held, sems):
    copies = [
        pltpu.make_async_copy(source, held, sems.at[i])
        for i, (source, held) in enumerate(
            ((ids, ids_held), (gate, gate_held), (tokens, tokens_held))
        )
    ]
    for copy in copies:
        copy.start()
    topk, block = ids.shape
    features = tokens.shape[1]
    wide = out.shape[1] - LANES
    if wide != features:
        out[...] = jnp.zeros_like(out)
    eye = lax.broadcasted_iota(jnp.int32, (block, block), 0) == lax.broadcasted_iota(
        jnp.int32, (block, block), 1
    )
    copies[0].wait()
    copies[1].wait()
    rows = jnp.concatenate(
        [
            ids_held[...].astype(F32),
            (gate_held[...] >> 8).astype(F32),
            (gate_held[...] & 255).astype(F32),
            jnp.zeros((LANES - 3 * topk, block), F32),
        ],
        axis=0,
    ).astype(BF16)
    out[:, wide:] = dot(jnp.where(eye, 1.0, 0.0).astype(BF16), rows, 1, 1).astype(BF16)
    copies[2].wait()
    out[:, :features] = tokens_held[...]


def pack_body(count, *refs):
    parts, out = refs[:count], refs[-1]
    at = 0
    for part in parts:
        out[at : at + part.shape[0]] = part[...]
        at += part.shape[0]


def pack(parts, after=(), passed=()):
    shape = (sum(p.shape[0] for p in parts), parts[0].shape[1])
    out = call(
        "pack",
        functools.partial(pack_body, len(parts)),
        [(shape, parts[0].dtype)],
        list(parts) + list(after),
        flops=1 << 29,
        passed=passed,
    )
    return out if passed else out[0]


def copy_body(source, after, out):
    out[...] = source[...]


def copied(source, after):
    return call("copied", copy_body, [(source.shape, source.dtype)], [source, after], 1 << 31)[0]


def inner_order():
    bits = bits_of("ingroup")
    return [
        sum(bit for i, bit in enumerate(bits) if k >> i & 1)
        for k in range(lax.axis_size("ingroup"))
    ]


def spread(own, cotangent):
    outer, inner = bits_of("group"), bits_of("ingroup")
    blocks = [own] + [swap(own, "ingroup", j) for j in inner_order()[1:]]
    half = len(blocks) // 2
    second = copied(cotangent, blocks[half])
    early = pack(blocks[:half])
    for bit in inner[:-1]:
        second = pack([second, swap(second, "ingroup", bit)])
    late = pack(blocks[half:], [early])
    across = swap(early, "group", outer[0])
    last = swap(late, "group", outer[0])
    first = pack([early, late, across, last], [second])
    for bit in outer[1:-1]:
        first = pack([first, swap(first, "group", bit)])
    first = [first, swap(first, "group", outer[-1])]
    return first, [second, swap(second, "ingroup", inner[-1])]


def spread_end(parts, after):
    held = [pack(parts, after)]
    for bit in bits_of("group"):
        held = held + [swap(part, "group", bit) for part in held]
    return held


def route_body(wide, topk, block, capacity, count, me, *refs):
    parts, (gate_weight, up_weight, place_out, scale_out, part_out, sent_out) = (
        refs[:count],
        refs[count:],
    )
    features = gate_weight.shape[0]
    total, slots = place_out.shape
    routing = jnp.concatenate([p[:, wide : wide + LANES] for p in parts], axis=0)
    lane = lax.broadcasted_iota(jnp.int32, (total, LANES), 1)
    match = (routing.astype(F32) == me[0].astype(F32)) & (lane < topk)
    source = lax.broadcasted_iota(jnp.int32, (LANES, LANES), 0)
    target = lax.broadcasted_iota(jnp.int32, (LANES, LANES), 1)

    def gate_half(offset):
        moved = dot(routing, jnp.where(source == target + offset, 1.0, 0.0).astype(BF16))
        own = jnp.where(match, moved, 0.0).astype(BF16)
        return dot(own, jnp.ones((LANES, LANES), BF16)).astype(BF16)

    named = dot(jnp.where(match, 1.0, 0.0).astype(BF16), jnp.ones((LANES, slots), BF16))
    chunk = min(total, CHUNK)
    row = lax.broadcasted_iota(jnp.int32, (chunk, chunk), 0)
    col = lax.broadcasted_iota(jnp.int32, (chunk, chunk), 1)
    earlier = jnp.where((row // block == col // block) & (row > col), 1.0, 0.0).astype(BF16)
    named_half = named.astype(BF16)
    rank = jnp.concatenate(
        [dot(earlier, named_half[i : i + chunk]) for i in range(0, total, chunk)], axis=0
    )
    start = lax.broadcasted_iota(jnp.int32, (total, slots), 0) // block * capacity
    slot = lax.broadcasted_iota(jnp.int32, (total, slots), 1) - start
    place = jnp.where((named > 0.5) & (rank == slot.astype(F32)), 1.0, 0.0).astype(BF16)
    place_out[...] = place
    high = dot(place, gate_half(topk), 0, 0)
    low = dot(place, gate_half(2 * topk), 0, 0)
    scale_out[...] = (high * 256.0 + low) / 65536.0
    values = jnp.concatenate([p[:, :features] for p in parts], axis=0)
    rows = dot(place, values, 0, 0).astype(BF16)
    for i, weight in enumerate((gate_weight, up_weight)):
        part = dot(rows, weight[...])
        part_out[i * slots : (i + 1) * slots] = part
        sent_out[i * slots : (i + 1) * slots] = part.astype(BF16)


def back_body(count, *refs):
    parts, (place, weight, part_out, sent_out) = refs[:count], refs[count:]
    values = jnp.concatenate([p[...] for p in parts], axis=0)
    rows = dot(place[...], values, 0, 0).astype(BF16)
    part = dot(rows, weight[...], 1, 1)
    part_out[...] = part
    sent_out[...] = part.astype(BF16)


def summed(own, received):
    total = own[...]
    for r in received:
        total = total + r[...].astype(F32)
    return total


def place_rows(place, rows, near_out, *far_outs):
    end = place.shape[0]
    for out in far_outs:
        start = end - out.shape[0]
        out[...] = dot(place[start:end], rows).astype(BF16)
        end = start
    near_out[...] = dot(place[:end], rows)


def forward_sums(both, received):
    total = summed(both, received)
    half = total.shape[0] // 2
    return total[:half], total[half:]


def out_body(peers, *refs):
    scale, place, weight, _, gate_out, up_out, *outs = refs[1 + peers :]
    gate_pre, up_pre = forward_sums(refs[0], refs[1 : 1 + peers])
    sigmoid = 1.0 / (1.0 + jnp.exp(-gate_pre))
    silu = gate_pre * sigmoid
    rows = (dot((silu * up_pre).astype(BF16), weight[...]) * scale[:, :1]).astype(BF16)
    place_rows(place[...], rows, *outs)
    scaled = sigmoid * scale[:, :1]
    gate_out[...] = up_pre * scaled * (1.0 + gate_pre * (1.0 - sigmoid))
    up_out[...] = silu * scale[:, :1]


def grad_body(peers, *refs):
    gate_factor, up_factor, back = refs[:3]
    gate_weight, up_weight, _, rows_out = refs[3 + peers :]
    d_hidden = summed(back, refs[3 : 3 + peers])
    d_gate = (d_hidden * gate_factor[...]).astype(BF16)
    d_up = (d_hidden * up_factor[...]).astype(BF16)
    rows_out[...] = (
        dot(d_gate, gate_weight[...], 1, 1) + dot(d_up, up_weight[...], 1, 1)
    ).astype(BF16)


def place_body(place, rows, near_out, go_out, stay_out):
    place_rows(place[...], rows[...], near_out, go_out, stay_out)


def step_body(block, near, go, keep, stay, received, far_out, keep_out, away_out):
    rows = far_out.shape[0]
    far_out[...] = (near[rows:] + go[...].astype(F32)).astype(BF16)
    half = keep_out.shape[0]
    total = keep[: 2 * half] + stay[...].astype(F32) + received[...].astype(F32)
    for at in range(0, half, block):
        keep_out[at : at + block] = total[2 * at : 2 * at + block]
        away_out[at : at + block] = total[2 * at + block : 2 * (at + block)].astype(BF16)


def join_body(near, stay, last, keep, got, own_out, mixed_out, pair_out, *away_outs):
    block = own_out.shape[0]
    rows = last.shape[0]
    total = near[:rows] + stay[:rows].astype(F32) + last[...].astype(F32)
    mixed = keep[...] + got[...].astype(F32)
    middle = rows // 2
    own_out[...] = total[:block]
    mixed_out[...] = mixed[:block]
    pair_out[:block] = mixed[block:].astype(BF16)
    pair_out[block:] = total[middle : middle + block].astype(BF16)
    starts = [at for at in range(block, rows, block) if at != middle]
    for at, out in zip(starts, away_outs):
        out[...] = total[at : at + block].astype(BF16)


def final_body(count, mixed, grad, pair, *refs):
    block = mixed.shape[0]
    mixed_out, grad_out = refs[count:]
    mixed_out[...] = (mixed[...] + pair[:block].astype(F32)).astype(BF16)
    grad_out[...] = (summed(grad, refs[:count]) + pair[block:].astype(F32)).astype(BF16)


def add_body(count, after, at, parts, keep, *refs):
    outs = refs[count + after :]
    rows = sum(out.shape[0] for out in outs)
    total = keep[at : at + rows].astype(F32)
    for received, start in zip(refs[:count], parts):
        total = total + received[start : start + rows].astype(F32)
    start = 0
    for out in outs:
        out[...] = total[start : start + out.shape[0]].astype(out.dtype)
        start += out.shape[0]


def far_body(keep, low, high, out):
    half = out.shape[0]
    middle = low.shape[0]
    out[:middle] = (keep[half : half + middle] + low[...].astype(F32)).astype(BF16)
    out[middle:] = (keep[half + middle :] + high[...].astype(F32)).astype(BF16)


def add(keep, at, received, outs, after=()):
    return call(
        "add",
        functools.partial(
            add_body, len(received), len(after), at, [start for _, start in received]
        ),
        [((rows, keep.shape[1]), dtype) for rows, dtype in outs],
        [keep] + [r for r, _ in received] + list(after),
    )


def collect_start(near, *pieces):
    for bit in reversed(bits_of("group")[2:]):
        half = near.shape[0] // 2
        got = jnp.concatenate([swap(piece, "group", bit) for piece in pieces[::-1]], axis=0)
        outs = [(piece.shape[0] // 2, BF16) for piece in pieces[::-1]]
        pieces = add(near, half, [(got, half)], outs)[::-1]
        (near,) = add(near, 0, [(got, 0)], [(half, F32)])
    return near, *[swap(piece, "group", bits_of("group")[1]) for piece in pieces]


def from_peers(sent):
    count = lax.axis_size("dp")
    return [
        lax.ppermute(sent, "dp", [(i, (i + step) % count) for i in range(count)])
        for step in range(1, count)
    ]


def on_device(tokens, cotangent, expert_ids, gate_fixed, w_gate, w_up, w_down):
    experts = lax.axis_size("group") * lax.axis_size("ingroup")
    block, features = tokens.shape
    topk = expert_ids.shape[1]
    hidden = w_gate.shape[2]
    capacity = 2 * block // lax.axis_size("ingroup")
    slots, total = experts * capacity, experts * block
    wide = -(-features // LANES) * LANES
    peers = lax.axis_size("dp") - 1
    w_gate, w_up, w_down = w_gate[0], w_up[0], w_down[0]
    product = 2 * slots * features * hidden

    me = lax.axis_index(PLANE).astype(jnp.int32).reshape(1)
    (own,) = call(
        "payload",
        payload_body,
        [((block, wide + LANES), BF16)],
        [me, tokens, expert_ids.T, gate_fixed.T],
        limit=58,
        hbm=(1, 2, 3),
        scratch=[pltpu.VMEM(tokens.shape, BF16)]
        + [pltpu.VMEM((topk, block), jnp.int32)] * 2
        + [pltpu.SemaphoreType.DMA((3,))],
    )
    x_parts, d_parts = spread(own, cotangent)
    both, both_sent = [((2 * slots, hidden), t) for t in (F32, BF16)]
    place, scale, both, both_sent = call(
        "forward",
        functools.partial(route_body, wide, topk, block, capacity, len(x_parts)),
        [((total, slots), BF16), ((slots, LANES), F32), both, both_sent],
        [me] + x_parts + [w_gate, w_up],
        2 * product,
        16,
    )
    both_in = from_peers(both_sent)
    d_parts = spread_end(d_parts, [both_sent])
    sums = [((slots, hidden), F32), ((slots, hidden), BF16)]
    back, back_sent = call(
        "back", functools.partial(back_body, len(d_parts)), sums, d_parts + [place, w_down], product
    )
    back_in = from_peers(back_sent)
    near = ((total // 2, features), F32)
    fourth, eighth = ((total // 4, features), BF16), ((total // 8, features), BF16)
    gate_factor, up_factor, *placed = call(
        "out",
        functools.partial(out_body, peers),
        [((slots, hidden), F32)] * 2 + [near, eighth, eighth, fourth],
        [both] + both_in + [scale, place, w_down, back_sent],
        product,
    )
    near_y, got_high, got_low, got_y = collect_start(*placed)
    half = near_y.shape[0] // 2
    (far,) = call(
        "add",
        far_body,
        [((half, features), BF16)],
        [near_y, got_low, got_high],
    )
    (rows,) = call(
        "grad",
        functools.partial(grad_body, peers),
        [((slots, features), BF16)],
        [gate_factor, up_factor, back] + back_in + [w_gate, w_up, far],
        2 * product,
        24,
    )
    axis, bits = "ingroup", bits_of("ingroup")
    count, across_bit = lax.axis_size("ingroup"), bits_of("group")[0]
    near_dx, got_go, got_dx = collect_start(
        *call("place", place_body, [near, fourth, fourth], [place, rows])
    )
    far, keep, away = call(
        "step",
        functools.partial(step_body, block),
        [((half, features), BF16)] + [((half // 2, features), t) for t in (F32, BF16)],
        [near_dx, got_go, near_y, got_y, swap(far, "group", across_bit)],
    )
    got = swap(away, axis, bits[0])
    for bit in bits[1:-1]:
        sums = (keep + got.astype(F32)).reshape(-1, 2, block, features)
        keep = sums[:, 0].reshape(-1, features)
        got = swap(sums[:, 1].reshape(-1, features).astype(BF16), axis, bit)
    own_dx, own_y, pair, *away = call(
        "join",
        join_body,
        [((block, features), F32)] * 2
        + [((2 * block, features), BF16)]
        + [((block, features), BF16)] * (count - 2),
        [near_dx, got_dx, swap(far, "group", across_bit), keep, got],
    )
    offsets = [j for j in inner_order() if j > 1]
    sent = [swap(part, axis, j) for j, part in zip(offsets, away)]
    outs = [((block, features), BF16)] * 2
    return call(
        "final",
        functools.partial(final_body, len(sent)),
        outs,
        [own_y, own_dx, swap(pair, axis, 1)] + sent,
    )


def solution(mesh):
    rows = P(PLANE, "dp")
    placed = (
        rows,
        rows,
        P(PLANE, None),
        P(PLANE, None),
        P(PLANE, "dp", None),
        P(PLANE, "dp", None),
        P(PLANE, None, "dp"),
    )
    return jax.shard_map(
        on_device, mesh=mesh, in_specs=placed, out_specs=(rows, rows), check_vma=False
    )
```

```python
import functools

import jax
import jax.numpy as jnp
from jax import lax
from jax.experimental import pallas as pl
from jax.experimental.pallas import tpu as pltpu
from jax.sharding import PartitionSpec as P

PLANE = ("group", "ingroup")
LANES = 128
CHUNK = 256
BF16 = jnp.bfloat16
F32 = jnp.float32


def dot(left, right, left_dim=1, right_dim=0):
    return lax.dot_general(
        left, right, (((left_dim,), (right_dim,)), ((), ())), preferred_element_type=F32
    )


def call(name, body, outs, args, flops=0, limit=16, hbm=(), passed=(), scratch=(), weight=1):
    shapes = [jax.ShapeDtypeStruct(shape, dtype) for shape, dtype in outs]
    moved = sum(a.size * a.dtype.itemsize for a in args)
    moved += sum(s.size * s.dtype.itemsize for s in shapes)
    specs = [
        pl.BlockSpec(
            memory_space=pltpu.HBM if i in hbm else pltpu.SMEM if a.shape == (1,) else pltpu.VMEM
        )
        for i, a in enumerate(args)
    ]
    inputs, results = len(args), len(shapes)

    def run(*refs):
        ins, rest = refs[:inputs], refs[inputs + len(passed) :]
        body(*ins, *rest[:results], *rest[results + len(passed) :])

    free = pl.BlockSpec(memory_space=pl.ANY)
    kernel = pl.pallas_call(
        run,
        out_shape=shapes + [jax.ShapeDtypeStruct(p.shape, p.dtype) for p in passed],
        in_specs=specs + [free] * len(passed),
        out_specs=[pl.BlockSpec(memory_space=pltpu.VMEM)] * results + [free] * len(passed),
        input_output_aliases={inputs + i: results + i for i in range(len(passed))},
        scratch_shapes=list(scratch),
        compiler_params=pltpu.CompilerParams(vmem_limit_bytes=limit << 20),
        name=name,
        cost_estimate=pl.CostEstimate(flops=flops, bytes_accessed=moved * weight, transcendentals=0),
    )
    with jax.named_scope(name):
        return kernel(*args, *passed)


def swap(value, axis, offset):
    return lax.ppermute(value, axis, [(i, i ^ offset) for i in range(lax.axis_size(axis))])


def bits_of(axis):
    bits, bit = [], lax.axis_size(axis) // 2
    while bit:
        bits.append(bit)
        bit //= 2
    return bits


def payload_body(me, tokens, ids, gate, out, tokens_held, ids_held, gate_held, sems):
    copies = [
        pltpu.make_async_copy(source, held, sems.at[i])
        for i, (source, held) in enumerate(
            ((ids, ids_held), (gate, gate_held), (tokens, tokens_held))
        )
    ]
    for copy in copies:
        copy.start()
    topk, block = ids.shape
    features = tokens.shape[1]
    wide = out.shape[1] - LANES
    if wide != features:
        out[...] = jnp.zeros_like(out)
    eye = lax.broadcasted_iota(jnp.int32, (block, block), 0) == lax.broadcasted_iota(
        jnp.int32, (block, block), 1
    )
    copies[0].wait()
    copies[1].wait()
    rows = jnp.concatenate(
        [
            ids_held[...].astype(F32),
            (gate_held[...] >> 8).astype(F32),
            (gate_held[...] & 255).astype(F32),
            jnp.zeros((LANES - 3 * topk, block), F32),
        ],
        axis=0,
    ).astype(BF16)
    out[:, wide:] = dot(jnp.where(eye, 1.0, 0.0).astype(BF16), rows, 1, 1).astype(BF16)
    copies[2].wait()
    out[:, :features] = tokens_held[...]


def pack_body(count, *refs):
    parts, out = refs[:count], refs[-1]
    at = 0
    for part in parts:
        out[at : at + part.shape[0]] = part[...]
        at += part.shape[0]


def pack(parts, after=(), passed=()):
    shape = (sum(p.shape[0] for p in parts), parts[0].shape[1])
    out = call(
        "pack",
        functools.partial(pack_body, len(parts)),
        [(shape, parts[0].dtype)],
        list(parts) + list(after),
        flops=1 << 29,
        passed=passed,
    )
    return out if passed else out[0]


def copy_body(source, after, out):
    out[...] = source[...]


def copied(source, after):
    return call("copied", copy_body, [(source.shape, source.dtype)], [source, after], 1 << 31)[0]


def inner_order():
    bits = bits_of("ingroup")
    return [
        sum(bit for i, bit in enumerate(bits) if k >> i & 1)
        for k in range(lax.axis_size("ingroup"))
    ]


def spread(own, cotangent):
    outer, inner = bits_of("group"), bits_of("ingroup")
    blocks = [own] + [swap(own, "ingroup", j) for j in inner_order()[1:]]
    half = len(blocks) // 2
    second = copied(cotangent, blocks[half])
    early = pack(blocks[:half])
    for bit in inner[:-1]:
        second = pack([second, swap(second, "ingroup", bit)])
    late = pack(blocks[half:], [early])
    across = swap(early, "group", outer[0])
    last = swap(late, "group", outer[0])
    first = pack([early, late, across, last], [second])
    for bit in outer[1:-1]:
        first = pack([first, swap(first, "group", bit)])
    first = [first, swap(first, "group", outer[-1])]
    return first, [second, swap(second, "ingroup", inner[-1])]


def spread_end(parts, after):
    held = [pack(parts, after)]
    for bit in bits_of("group"):
        held = held + [swap(part, "group", bit) for part in held]
    return held


def route_body(wide, topk, block, capacity, count, me, *refs):
    parts, (gate_weight, up_weight, place_out, scale_out, part_out, sent_out) = (
        refs[:count],
        refs[count:],
    )
    features = gate_weight.shape[0]
    total, slots = place_out.shape
    routing = jnp.concatenate([p[:, wide : wide + LANES] for p in parts], axis=0)
    lane = lax.broadcasted_iota(jnp.int32, (total, LANES), 1)
    match = (routing.astype(F32) == me[0].astype(F32)) & (lane < topk)
    source = lax.broadcasted_iota(jnp.int32, (LANES, LANES), 0)
    target = lax.broadcasted_iota(jnp.int32, (LANES, LANES), 1)

    def gate_half(offset):
        moved = dot(routing, jnp.where(source == target + offset, 1.0, 0.0).astype(BF16))
        own = jnp.where(match, moved, 0.0).astype(BF16)
        return dot(own, jnp.ones((LANES, LANES), BF16)).astype(BF16)

    named = dot(jnp.where(match, 1.0, 0.0).astype(BF16), jnp.ones((LANES, slots), BF16))
    chunk = min(total, CHUNK)
    row = lax.broadcasted_iota(jnp.int32, (chunk, chunk), 0)
    col = lax.broadcasted_iota(jnp.int32, (chunk, chunk), 1)
    earlier = jnp.where((row // block == col // block) & (row > col), 1.0, 0.0).astype(BF16)
    named_half = named.astype(BF16)
    rank = jnp.concatenate(
        [dot(earlier, named_half[i : i + chunk]) for i in range(0, total, chunk)], axis=0
    )
    start = lax.broadcasted_iota(jnp.int32, (total, slots), 0) // block * capacity
    slot = lax.broadcasted_iota(jnp.int32, (total, slots), 1) - start
    place = jnp.where((named > 0.5) & (rank == slot.astype(F32)), 1.0, 0.0).astype(BF16)
    place_out[...] = place
    high = dot(place, gate_half(topk), 0, 0)
    low = dot(place, gate_half(2 * topk), 0, 0)
    scale_out[...] = (high * 256.0 + low) / 65536.0
    values = jnp.concatenate([p[:, :features] for p in parts], axis=0)
    rows = dot(place, values, 0, 0).astype(BF16)
    for i, weight in enumerate((gate_weight, up_weight)):
        part = dot(rows, weight[...])
        part_out[i * slots : (i + 1) * slots] = part
        sent_out[i * slots : (i + 1) * slots] = part.astype(BF16)


def back_body(count, *refs):
    parts, (place, weight, part_out, sent_out) = refs[:count], refs[count:]
    values = jnp.concatenate([p[...] for p in parts], axis=0)
    rows = dot(place[...], values, 0, 0).astype(BF16)
    part = dot(rows, weight[...], 1, 1)
    part_out[...] = part
    sent_out[...] = part.astype(BF16)


def summed(own, received):
    total = own[...]
    for r in received:
        total = total + r[...].astype(F32)
    return total


def place_rows(place, rows, near_out, *far_outs):
    end = place.shape[0]
    for out in far_outs:
        start = end - out.shape[0]
        out[...] = dot(place[start:end], rows).astype(BF16)
        end = start
    near_out[...] = dot(place[:end], rows)


def forward_sums(both, received):
    total = summed(both, received)
    half = total.shape[0] // 2
    return total[:half], total[half:]


def out_body(peers, *refs):
    scale, place, weight, _, gate_out, up_out, *outs = refs[1 + peers :]
    gate_pre, up_pre = forward_sums(refs[0], refs[1 : 1 + peers])
    sigmoid = 1.0 / (1.0 + jnp.exp(-gate_pre))
    silu = gate_pre * sigmoid
    rows = (dot((silu * up_pre).astype(BF16), weight[...]) * scale[:, :1]).astype(BF16)
    place_rows(place[...], rows, *outs)
    scaled = sigmoid * scale[:, :1]
    gate_out[...] = up_pre * scaled * (1.0 + gate_pre * (1.0 - sigmoid))
    up_out[...] = silu * scale[:, :1]


def grad_body(peers, *refs):
    gate_factor, up_factor, back = refs[:3]
    gate_weight, up_weight, _, rows_out = refs[3 + peers :]
    d_hidden = summed(back, refs[3 : 3 + peers])
    d_gate = (d_hidden * gate_factor[...]).astype(BF16)
    d_up = (d_hidden * up_factor[...]).astype(BF16)
    rows_out[...] = (
        dot(d_gate, gate_weight[...], 1, 1) + dot(d_up, up_weight[...], 1, 1)
    ).astype(BF16)


def place_body(place, rows, keep, stay, received, near_out, go_out, stay_out, keep_out, far_out):
    place_rows(place[...], rows[...], near_out, go_out, stay_out)
    half = keep_out.shape[0]
    total = keep[: 2 * half] + stay[...].astype(F32) + received[...].astype(F32)
    keep_out[...] = total[:half]
    far_out[...] = total[half:].astype(BF16)


def join_body(near, stay, last, keep, got, own_out, mixed_out, pair_out, *away_outs):
    block = own_out.shape[0]
    rows = last.shape[0]
    total = near[:rows] + stay[:rows].astype(F32) + last[...].astype(F32)
    mixed = keep[...] + got[...].astype(F32)
    own_out[...] = total[:block]
    mixed_out[...] = mixed[:block]
    pair_out[:block] = mixed[block:].astype(BF16)
    pair_out[block:] = total[block : 2 * block].astype(BF16)
    for at, out in zip(range(2 * block, rows, block), away_outs):
        out[...] = total[at : at + block].astype(BF16)


def final_body(count, mixed, grad, pair, *refs):
    block = mixed.shape[0]
    mixed_out, grad_out = refs[count:]
    mixed_out[...] = (mixed[...] + pair[:block].astype(F32)).astype(BF16)
    grad_out[...] = (summed(grad, refs[:count]) + pair[block:].astype(F32)).astype(BF16)


def add_body(count, after, at, parts, keep, *refs):
    outs = refs[count + after :]
    rows = sum(out.shape[0] for out in outs)
    total = keep[at : at + rows].astype(F32)
    for received, start in zip(refs[:count], parts):
        total = total + received[start : start + rows].astype(F32)
    start = 0
    for out in outs:
        out[...] = total[start : start + out.shape[0]].astype(out.dtype)
        start += out.shape[0]


def far_body(keep, low, high, out):
    half = out.shape[0]
    middle = low.shape[0]
    out[:middle] = (keep[half : half + middle] + low[...].astype(F32)).astype(BF16)
    out[middle:] = (keep[half + middle :] + high[...].astype(F32)).astype(BF16)


def add(keep, at, received, outs, after=()):
    return call(
        "add",
        functools.partial(
            add_body, len(received), len(after), at, [start for _, start in received]
        ),
        [((rows, keep.shape[1]), dtype) for rows, dtype in outs],
        [keep] + [r for r, _ in received] + list(after),
    )


def collect_start(near, *pieces):
    for bit in reversed(bits_of("group")[2:]):
        half = near.shape[0] // 2
        got = jnp.concatenate([swap(piece, "group", bit) for piece in pieces[::-1]], axis=0)
        outs = [(piece.shape[0] // 2, BF16) for piece in pieces[::-1]]
        pieces = add(near, half, [(got, half)], outs)[::-1]
        (near,) = add(near, 0, [(got, 0)], [(half, F32)])
    return near, *[swap(piece, "group", bits_of("group")[1]) for piece in pieces]


def from_peers(sent):
    count = lax.axis_size("dp")
    return [
        lax.ppermute(sent, "dp", [(i, (i + step) % count) for i in range(count)])
        for step in range(1, count)
    ]


def on_device(tokens, cotangent, expert_ids, gate_fixed, w_gate, w_up, w_down):
    experts = lax.axis_size("group") * lax.axis_size("ingroup")
    block, features = tokens.shape
    topk = expert_ids.shape[1]
    hidden = w_gate.shape[2]
    capacity = 2 * block // lax.axis_size("ingroup")
    slots, total = experts * capacity, experts * block
    wide = -(-features // LANES) * LANES
    peers = lax.axis_size("dp") - 1
    w_gate, w_up, w_down = w_gate[0], w_up[0], w_down[0]
    product = 2 * slots * features * hidden

    me = lax.axis_index(PLANE).astype(jnp.int32).reshape(1)
    (own,) = call(
        "payload",
        payload_body,
        [((block, wide + LANES), BF16)],
        [me, tokens, expert_ids.T, gate_fixed.T],
        limit=58,
        hbm=(1, 2, 3),
        scratch=[pltpu.VMEM(tokens.shape, BF16)]
        + [pltpu.VMEM((topk, block), jnp.int32)] * 2
        + [pltpu.SemaphoreType.DMA((3,))],
    )
    x_parts, d_parts = spread(own, cotangent)
    both, both_sent = [((2 * slots, hidden), t) for t in (F32, BF16)]
    place, scale, both, both_sent = call(
        "forward",
        functools.partial(route_body, wide, topk, block, capacity, len(x_parts)),
        [((total, slots), BF16), ((slots, LANES), F32), both, both_sent],
        [me] + x_parts + [w_gate, w_up],
        2 * product,
        16,
    )
    both_in = from_peers(both_sent)
    d_parts = spread_end(d_parts, [both_sent])
    sums = [((slots, hidden), F32), ((slots, hidden), BF16)]
    back, back_sent = call(
        "back", functools.partial(back_body, len(d_parts)), sums, d_parts + [place, w_down], product
    )
    back_in = from_peers(back_sent)
    near = ((total // 2, features), F32)
    fourth, eighth = ((total // 4, features), BF16), ((total // 8, features), BF16)
    gate_factor, up_factor, *placed = call(
        "out",
        functools.partial(out_body, peers),
        [((slots, hidden), F32)] * 2 + [near, eighth, eighth, fourth],
        [both] + both_in + [scale, place, w_down, back_sent],
        product,
    )
    near_y, got_high, got_low, got_y = collect_start(*placed)
    half = near_y.shape[0] // 2
    (far,) = call(
        "add",
        far_body,
        [((half, features), BF16)],
        [near_y, got_low, got_high],
    )
    (rows,) = call(
        "grad",
        functools.partial(grad_body, peers),
        [((slots, features), BF16)],
        [gate_factor, up_factor, back] + back_in + [w_gate, w_up, far],
        2 * product,
        24,
    )
    axis, bits = "ingroup", bits_of("ingroup")
    count, across_bit = lax.axis_size("ingroup"), bits_of("group")[0]
    near_dx, go, stay, keep, far = call(
        "place",
        place_body,
        [near, fourth, fourth] + [((half // 2, features), t) for t in (F32, BF16)],
        [place, rows, near_y, got_y, swap(far, "group", across_bit)],
    )
    near_dx, got_go, got_dx = collect_start(near_dx, go, stay)
    got = swap(far, axis, bits[-1])
    for bit in bits[-2:0:-1]:
        outs = [(keep.shape[0] // 2, t) for t in (F32, BF16)]
        keep, away = add(keep, 0, [(got, 0)], outs)
        got = swap(away, axis, bit)
    (far,) = add(near_dx, half, [(got_go, 0)], [(half, BF16)])
    own_dx, own_y, pair, *away = call(
        "join",
        join_body,
        [((block, features), F32)] * 2
        + [((2 * block, features), BF16)]
        + [((block, features), BF16)] * (count - 2),
        [near_dx, got_dx, swap(far, "group", across_bit), keep, got],
    )
    sent = [swap(part, axis, j) for j, part in zip(inner_order()[2:], away)]
    outs = [((block, features), BF16)] * 2
    return call(
        "final",
        functools.partial(final_body, len(sent)),
        outs,
        [own_y, own_dx, swap(pair, axis, bits[0])] + sent,
    )


def solution(mesh):
    rows = P(PLANE, "dp")
    placed = (
        rows,
        rows,
        P(PLANE, None),
        P(PLANE, None),
        P(PLANE, "dp", None),
        P(PLANE, "dp", None),
        P(PLANE, None, "dp"),
    )
    return jax.shard_map(
        on_device, mesh=mesh, in_specs=placed, out_specs=(rows, rows), check_vma=False
    )
```

```python
import functools

import jax
import jax.numpy as jnp
from jax import lax
from jax.experimental import pallas as pl
from jax.experimental.pallas import tpu as pltpu
from jax.sharding import PartitionSpec as P

PLANE = ("group", "ingroup")
LANES = 128
CHUNK = 256
BF16 = jnp.bfloat16
F32 = jnp.float32


def dot(left, right, left_dim=1, right_dim=0):
    return lax.dot_general(
        left, right, (((left_dim,), (right_dim,)), ((), ())), preferred_element_type=F32
    )


def call(name, body, outs, args, flops=0, limit=16, hbm=(), passed=(), scratch=(), weight=1):
    shapes = [jax.ShapeDtypeStruct(shape, dtype) for shape, dtype in outs]
    moved = sum(a.size * a.dtype.itemsize for a in args)
    moved += sum(s.size * s.dtype.itemsize for s in shapes)
    specs = [
        pl.BlockSpec(
            memory_space=pltpu.HBM if i in hbm else pltpu.SMEM if a.shape == (1,) else pltpu.VMEM
        )
        for i, a in enumerate(args)
    ]
    inputs, results = len(args), len(shapes)

    def run(*refs):
        ins, rest = refs[:inputs], refs[inputs + len(passed) :]
        body(*ins, *rest[:results], *rest[results + len(passed) :])

    free = pl.BlockSpec(memory_space=pl.ANY)
    kernel = pl.pallas_call(
        run,
        out_shape=shapes + [jax.ShapeDtypeStruct(p.shape, p.dtype) for p in passed],
        in_specs=specs + [free] * len(passed),
        out_specs=[pl.BlockSpec(memory_space=pltpu.VMEM)] * results + [free] * len(passed),
        input_output_aliases={inputs + i: results + i for i in range(len(passed))},
        scratch_shapes=list(scratch),
        compiler_params=pltpu.CompilerParams(vmem_limit_bytes=limit << 20),
        name=name,
        cost_estimate=pl.CostEstimate(flops=flops, bytes_accessed=moved * weight, transcendentals=0),
    )
    with jax.named_scope(name):
        return kernel(*args, *passed)


def swap(value, axis, offset):
    return lax.ppermute(value, axis, [(i, i ^ offset) for i in range(lax.axis_size(axis))])


def bits_of(axis):
    bits, bit = [], lax.axis_size(axis) // 2
    while bit:
        bits.append(bit)
        bit //= 2
    return bits


def payload_body(me, tokens, ids, gate, out, tokens_held, ids_held, gate_held, sems):
    topk, block = ids.shape
    features = tokens.shape[1]
    wide = out.shape[1] - LANES
    place = tokens_held if wide != features else out.at[:, pl.ds(0, features)]
    copies = [
        pltpu.make_async_copy(source, held, sems.at[i])
        for i, (source, held) in enumerate(((ids, ids_held), (gate, gate_held), (tokens, place)))
    ]
    for copy in copies:
        copy.start()
    if wide != features:
        out[...] = jnp.zeros_like(out)
    eye = lax.broadcasted_iota(jnp.int32, (block, block), 0) == lax.broadcasted_iota(
        jnp.int32, (block, block), 1
    )
    copies[0].wait()
    copies[1].wait()
    rows = jnp.concatenate(
        [
            ids_held[...].astype(F32),
            (gate_held[...] >> 8).astype(F32),
            (gate_held[...] & 255).astype(F32),
            jnp.zeros((LANES - 3 * topk, block), F32),
        ],
        axis=0,
    ).astype(BF16)
    out[:, wide:] = dot(jnp.where(eye, 1.0, 0.0).astype(BF16), rows, 1, 1).astype(BF16)
    copies[2].wait()
    if wide != features:
        out[:, :features] = tokens_held[...]


def pack_body(count, *refs):
    parts, out = refs[:count], refs[-1]
    at = 0
    for part in parts:
        out[at : at + part.shape[0]] = part[...]
        at += part.shape[0]


def pack(parts, after=(), passed=()):
    shape = (sum(p.shape[0] for p in parts), parts[0].shape[1])
    out = call(
        "pack",
        functools.partial(pack_body, len(parts)),
        [(shape, parts[0].dtype)],
        list(parts) + list(after),
        flops=1 << 29,
        passed=passed,
    )
    return out if passed else out[0]


def copy_body(source, after, out):
    out[...] = source[...]


def copied(source, after):
    return call("copied", copy_body, [(source.shape, source.dtype)], [source, after], 1 << 31)[0]


def inner_order():
    bits = bits_of("ingroup")
    return [
        sum(bit for i, bit in enumerate(bits) if k >> i & 1)
        for k in range(lax.axis_size("ingroup"))
    ]


def spread(own, cotangent):
    outer, inner = bits_of("group"), bits_of("ingroup")
    blocks = [own] + [swap(own, "ingroup", j) for j in inner_order()[1:]]
    half = len(blocks) // 2
    second = copied(cotangent, blocks[half])
    early = pack(blocks[:half])
    for bit in inner[:-1]:
        second = pack([second, swap(second, "ingroup", bit)])
    late = pack(blocks[half:], [early])
    across = swap(early, "group", outer[0])
    last = swap(late, "group", outer[0])
    first = pack([early, late, across, last], [second])
    for bit in outer[1:-1]:
        first = pack([first, swap(first, "group", bit)])
    first = [first, swap(first, "group", outer[-1])]
    return first, [second, swap(second, "ingroup", inner[-1])]


def spread_end(parts, after):
    held = [pack(parts, after)]
    for bit in bits_of("group"):
        held = held + [swap(part, "group", bit) for part in held]
    return held


def route_body(wide, topk, block, capacity, count, me, *refs):
    parts, (gate_weight, up_weight, place_out, scale_out, part_out, sent_out) = (
        refs[:count],
        refs[count:],
    )
    features = gate_weight.shape[0]
    total, slots = place_out.shape
    routing = jnp.concatenate([p[:, wide : wide + LANES] for p in parts], axis=0)
    lane = lax.broadcasted_iota(jnp.int32, (total, LANES), 1)
    match = (routing.astype(F32) == me[0].astype(F32)) & (lane < topk)
    source = lax.broadcasted_iota(jnp.int32, (LANES, LANES), 0)
    target = lax.broadcasted_iota(jnp.int32, (LANES, LANES), 1)

    def gate_half(offset):
        moved = dot(routing, jnp.where(source == target + offset, 1.0, 0.0).astype(BF16))
        own = jnp.where(match, moved, 0.0).astype(BF16)
        return dot(own, jnp.ones((LANES, LANES), BF16)).astype(BF16)

    named = dot(jnp.where(match, 1.0, 0.0).astype(BF16), jnp.ones((LANES, slots), BF16))
    chunk = min(total, CHUNK)
    row = lax.broadcasted_iota(jnp.int32, (chunk, chunk), 0)
    col = lax.broadcasted_iota(jnp.int32, (chunk, chunk), 1)
    earlier = jnp.where((row // block == col // block) & (row > col), 1.0, 0.0).astype(BF16)
    named_half = named.astype(BF16)
    rank = jnp.concatenate(
        [dot(earlier, named_half[i : i + chunk]) for i in range(0, total, chunk)], axis=0
    )
    start = lax.broadcasted_iota(jnp.int32, (total, slots), 0) // block * capacity
    slot = lax.broadcasted_iota(jnp.int32, (total, slots), 1) - start
    place = jnp.where((named > 0.5) & (rank == slot.astype(F32)), 1.0, 0.0).astype(BF16)
    place_out[...] = place
    high = dot(place, gate_half(topk), 0, 0)
    low = dot(place, gate_half(2 * topk), 0, 0)
    scale_out[...] = (high * 256.0 + low) / 65536.0
    values = jnp.concatenate([p[:, :features] for p in parts], axis=0)
    rows = dot(place, values, 0, 0).astype(BF16)
    for i, weight in enumerate((gate_weight, up_weight)):
        part = dot(rows, weight[...])
        part_out[i * slots : (i + 1) * slots] = part
        sent_out[i * slots : (i + 1) * slots] = part.astype(BF16)


def back_body(count, *refs):
    parts, (place, weight, part_out, sent_out) = refs[:count], refs[count:]
    values = jnp.concatenate([p[...] for p in parts], axis=0)
    rows = dot(place[...], values, 0, 0).astype(BF16)
    part = dot(rows, weight[...], 1, 1)
    part_out[...] = part
    sent_out[...] = part.astype(BF16)


def summed(own, received):
    total = own[...]
    for r in received:
        total = total + r[...].astype(F32)
    return total


def place_rows(place, rows, near_out, *far_outs):
    end = place.shape[0]
    for out in far_outs:
        start = end - out.shape[0]
        out[...] = dot(place[start:end], rows).astype(BF16)
        end = start
    near_out[...] = dot(place[:end], rows)


def forward_sums(both, received):
    total = summed(both, received)
    half = total.shape[0] // 2
    return total[:half], total[half:]


def out_body(peers, *refs):
    scale, place, weight, _, gate_out, up_out, *outs = refs[1 + peers :]
    gate_pre, up_pre = forward_sums(refs[0], refs[1 : 1 + peers])
    sigmoid = 1.0 / (1.0 + jnp.exp(-gate_pre))
    silu = gate_pre * sigmoid
    rows = (dot((silu * up_pre).astype(BF16), weight[...]) * scale[:, :1]).astype(BF16)
    place_rows(place[...], rows, *outs)
    scaled = sigmoid * scale[:, :1]
    gate_out[...] = up_pre * scaled * (1.0 + gate_pre * (1.0 - sigmoid))
    up_out[...] = silu * scale[:, :1]


def grad_body(peers, *refs):
    gate_factor, up_factor, back = refs[:3]
    gate_weight, up_weight, _, rows_out = refs[3 + peers :]
    d_hidden = summed(back, refs[3 : 3 + peers])
    d_gate = (d_hidden * gate_factor[...]).astype(BF16)
    d_up = (d_hidden * up_factor[...]).astype(BF16)
    rows_out[...] = (
        dot(d_gate, gate_weight[...], 1, 1) + dot(d_up, up_weight[...], 1, 1)
    ).astype(BF16)


def place_body(place, rows, keep, stay, received, near_out, go_out, stay_out, keep_out, far_out):
    place_rows(place[...], rows[...], near_out, go_out, stay_out)
    half = keep_out.shape[0]
    total = keep[: 2 * half] + stay[...].astype(F32) + received[...].astype(F32)
    keep_out[...] = total[:half]
    far_out[...] = total[half:].astype(BF16)


def join_body(near, stay, last, keep, got, own_out, mixed_out, pair_out, *away_outs):
    block = own_out.shape[0]
    rows = last.shape[0]
    total = near[:rows] + stay[:rows].astype(F32) + last[...].astype(F32)
    mixed = keep[...] + got[...].astype(F32)
    own_out[...] = total[:block]
    mixed_out[...] = mixed[:block]
    pair_out[:block] = mixed[block:].astype(BF16)
    pair_out[block:] = total[block : 2 * block].astype(BF16)
    for at, out in zip(range(2 * block, rows, block), away_outs):
        out[...] = total[at : at + block].astype(BF16)


def final_body(count, mixed, grad, pair, *refs):
    block = mixed.shape[0]
    mixed_out, grad_out = refs[count:]
    mixed_out[...] = (mixed[...] + pair[:block].astype(F32)).astype(BF16)
    grad_out[...] = (summed(grad, refs[:count]) + pair[block:].astype(F32)).astype(BF16)


def add_body(count, after, at, parts, keep, *refs):
    outs = refs[count + after :]
    rows = sum(out.shape[0] for out in outs)
    total = keep[at : at + rows].astype(F32)
    for received, start in zip(refs[:count], parts):
        total = total + received[start : start + rows].astype(F32)
    start = 0
    for out in outs:
        out[...] = total[start : start + out.shape[0]].astype(out.dtype)
        start += out.shape[0]


def far_body(keep, low, high, out):
    half = out.shape[0]
    middle = low.shape[0]
    out[:middle] = (keep[half : half + middle] + low[...].astype(F32)).astype(BF16)
    out[middle:] = (keep[half + middle :] + high[...].astype(F32)).astype(BF16)


def add(keep, at, received, outs, after=()):
    return call(
        "add",
        functools.partial(
            add_body, len(received), len(after), at, [start for _, start in received]
        ),
        [((rows, keep.shape[1]), dtype) for rows, dtype in outs],
        [keep] + [r for r, _ in received] + list(after),
    )


def collect_start(near, *pieces):
    for bit in reversed(bits_of("group")[2:]):
        half = near.shape[0] // 2
        got = jnp.concatenate([swap(piece, "group", bit) for piece in pieces[::-1]], axis=0)
        outs = [(piece.shape[0] // 2, BF16) for piece in pieces[::-1]]
        pieces = add(near, half, [(got, half)], outs)[::-1]
        (near,) = add(near, 0, [(got, 0)], [(half, F32)])
    return near, *[swap(piece, "group", bits_of("group")[1]) for piece in pieces]


def from_peers(sent):
    count = lax.axis_size("dp")
    return [
        lax.ppermute(sent, "dp", [(i, (i + step) % count) for i in range(count)])
        for step in range(1, count)
    ]


def on_device(tokens, cotangent, expert_ids, gate_fixed, w_gate, w_up, w_down):
    experts = lax.axis_size("group") * lax.axis_size("ingroup")
    block, features = tokens.shape
    topk = expert_ids.shape[1]
    hidden = w_gate.shape[2]
    capacity = 2 * block // lax.axis_size("ingroup")
    slots, total = experts * capacity, experts * block
    wide = -(-features // LANES) * LANES
    peers = lax.axis_size("dp") - 1
    w_gate, w_up, w_down = w_gate[0], w_up[0], w_down[0]
    product = 2 * slots * features * hidden

    me = lax.axis_index(PLANE).astype(jnp.int32).reshape(1)
    (own,) = call(
        "payload",
        payload_body,
        [((block, wide + LANES), BF16)],
        [me, tokens, expert_ids.T, gate_fixed.T],
        limit=58,
        hbm=(1, 2, 3),
        scratch=[pltpu.VMEM(tokens.shape, BF16)]
        + [pltpu.VMEM((topk, block), jnp.int32)] * 2
        + [pltpu.SemaphoreType.DMA((3,))],
    )
    x_parts, d_parts = spread(own, cotangent)
    both, both_sent = [((2 * slots, hidden), t) for t in (F32, BF16)]
    place, scale, both, both_sent = call(
        "forward",
        functools.partial(route_body, wide, topk, block, capacity, len(x_parts)),
        [((total, slots), BF16), ((slots, LANES), F32), both, both_sent],
        [me] + x_parts + [w_gate, w_up],
        2 * product,
        16,
    )
    both_in = from_peers(both_sent)
    d_parts = spread_end(d_parts, [both_sent])
    sums = [((slots, hidden), F32), ((slots, hidden), BF16)]
    back, back_sent = call(
        "back", functools.partial(back_body, len(d_parts)), sums, d_parts + [place, w_down], product
    )
    back_in = from_peers(back_sent)
    near = ((total // 2, features), F32)
    fourth, eighth = ((total // 4, features), BF16), ((total // 8, features), BF16)
    gate_factor, up_factor, *placed = call(
        "out",
        functools.partial(out_body, peers),
        [((slots, hidden), F32)] * 2 + [near, eighth, eighth, fourth],
        [both] + both_in + [scale, place, w_down, back_sent],
        product,
    )
    near_y, got_high, got_low, got_y = collect_start(*placed)
    half = near_y.shape[0] // 2
    (far,) = call(
        "add",
        far_body,
        [((half, features), BF16)],
        [near_y, got_low, got_high],
    )
    (rows,) = call(
        "grad",
        functools.partial(grad_body, peers),
        [((slots, features), BF16)],
        [gate_factor, up_factor, back] + back_in + [w_gate, w_up, far],
        2 * product,
        24,
    )
    axis, bits = "ingroup", bits_of("ingroup")
    count, across_bit = lax.axis_size("ingroup"), bits_of("group")[0]
    near_dx, go, stay, keep, far = call(
        "place",
        place_body,
        [near, fourth, fourth] + [((half // 2, features), t) for t in (F32, BF16)],
        [place, rows, near_y, got_y, swap(far, "group", across_bit)],
    )
    near_dx, got_go, got_dx = collect_start(near_dx, go, stay)
    got = swap(far, axis, bits[-1])
    for bit in bits[-2:0:-1]:
        outs = [(keep.shape[0] // 2, t) for t in (F32, BF16)]
        keep, away = add(keep, 0, [(got, 0)], outs)
        got = swap(away, axis, bit)
    (far,) = add(near_dx, half, [(got_go, 0)], [(half, BF16)])
    own_dx, own_y, pair, *away = call(
        "join",
        join_body,
        [((block, features), F32)] * 2
        + [((2 * block, features), BF16)]
        + [((block, features), BF16)] * (count - 2),
        [near_dx, got_dx, swap(far, "group", across_bit), keep, got],
    )
    sent = [swap(part, axis, j) for j, part in zip(inner_order()[2:], away)]
    outs = [((block, features), BF16)] * 2
    return call(
        "final",
        functools.partial(final_body, len(sent)),
        outs,
        [own_y, own_dx, swap(pair, axis, bits[0])] + sent,
    )


def solution(mesh):
    rows = P(PLANE, "dp")
    placed = (
        rows,
        rows,
        P(PLANE, None),
        P(PLANE, None),
        P(PLANE, "dp", None),
        P(PLANE, "dp", None),
        P(PLANE, None, "dp"),
    )
    return jax.shard_map(
        on_device, mesh=mesh, in_specs=placed, out_specs=(rows, rows), check_vma=False
    )
```
